32 devices in a mesh: fsdp: 8 (over z, y), seq: 4 (over x, core).
Axes of the slice: x: 2, y: 2, z: 4, core: 2. Of those that a mesh axis runs over, the one named last changes fastest.
Arguments:
- text_embeds: bfloat16 [2240, 4096], P('fsdp'), may hold values from -8 to 8
- vision_tokens: bfloat16 [1024, 4096], P('fsdp', 'seq'), may hold values from -6 to 6
- vision_request: int32 [1024, 1], P('fsdp'), may hold values from 0 to 7; in each aligned block of 128 rows (0 to 127, 128 to 255, ...) at most 32 rows name the same one
- image_start: int32 [8], P('fsdp'), may hold values from 1 to 16
- lengths: int32 [8], P('fsdp'), may hold values from 273 to 280
- attn_gain: float32 [4096], replicated, may hold values from 0.5 to 1.5
- w_query: bfloat16 [4096, 2048], P('fsdp', 'seq'), may hold values from -1 to 1
- w_key: bfloat16 [4096, 2048], P('fsdp', 'seq'), may hold values from -1 to 1
- w_value: bfloat16 [4096, 2048], P('fsdp', 'seq'), may hold values from -0.09375 to 0.09375
- w_out: bfloat16 [2048, 4096], P(None, 'fsdp'), may hold values from -0.125 to 0.125
- final_gain: float32 [4096], replicated, may hold values from 0.25 to 1.75
- lm_head: bfloat16 [4096, 32000], P(None, 'fsdp'), may hold values from -0.25 to 0.25
Outputs:
- state_rms: float32 [8], P('seq')
- max_logit: float32 [8], P('seq')
The draws below stay inside these ranges and needn't reach their ends.
Inputs may be any that keep to these rules, and one draw needn't show every extreme that they name: `vision_request`: within the 128 vision tokens of one index of fsdp no request is named more than 32 times, a bound that some block reaches; every request is named by some vision token. `lengths`: each request's image tokens end before its last token.
All inputs are finite; a program needn't handle non-finite values.
Results may differ from the reference program's by a relative error of at most 0.0024.
Values may be sent and summed in bfloat16 or wider, within the bound.
A program may use at most 128 MiB of HBM per device.

```python
import math
import jax
import jax.numpy as jnp
import numpy as np
from jax import lax

D = 4096
HD = 128
VOCAB = 32000
HEADS = 16
VT_GRP = 128
SEQ_LEN = 280
REQUESTS = 8
VTOK = 1024
CAP = 32
IMG_MAX = 256
ATTN = 2048


def column_scale():
    return 0.6 + 1.2 * jnp.arange(D, dtype=jnp.float32) / D


def draw_text_embeds(key, part):
    noise = jax.random.normal(jax.random.fold_in(key, 11), (REQUESTS * SEQ_LEN, D), jnp.float32)
    rows = noise
    return jnp.clip(rows * column_scale()[None, :], -8.0, 8.0).astype(jnp.bfloat16)


def draw_w_query(key, part):
    noise = jax.random.normal(jax.random.fold_in(key, 1), (D, HEADS * HD), jnp.float32) * math.sqrt(2.0 / D)
    weights = noise
    return jnp.clip(weights, -1.0, 1.0).astype(jnp.bfloat16)


def draw_w_key(key, part):
    noise = jax.random.normal(jax.random.fold_in(key, 2), (D, HEADS * HD), jnp.float32) * math.sqrt(2.0 / D)
    weights = noise
    return jnp.clip(weights, -1.0, 1.0).astype(jnp.bfloat16)


def with_ends(values, key, smallest, high):
    extent = values.shape
    index_at = [jax.random.randint(jax.random.fold_in(key, axis), (), 0, extent[axis]) for axis in range(len(extent))]
    values = values.at[tuple(index_at)].set(smallest)
    longest = extent.index(max(extent))
    index_at[longest] = (index_at[longest] + 1) % extent[longest]
    return values.at[tuple(index_at)].set(high)


def steps_of(key, shape, pieces, smallest, high):
    gain = 1.0
    for dim, parts in pieces:
        draws = jax.random.uniform(jax.random.fold_in(jax.random.fold_in(key, 6), dim), (parts,), jnp.float32, smallest / len(pieces), high / len(pieces))
        gain = gain * jnp.repeat(jnp.exp(draws), shape[dim] // parts).reshape((-1,) + (1,) * (len(shape) - 1 - dim))
    return gain


def deal_out(own_key, own, number, rows, amount, top, bound, lean):
    order = jax.random.permutation(own_key, amount)
    heavy_load, ordinary = load_shares(amount, rows * top, bound, lean, True), load_shares(amount, rows * top, bound, lean, False)
    places = jnp.arange(amount)

    def named(tallies, rotation):
        used = int((tallies > 0).sum())
        fixed = max(1, used // 4)
        moved = fixed + (places - fixed + rotation * (used - fixed)) % max(1, amount - fixed)
        return jnp.zeros((amount,), jnp.int32).at[order[jnp.where(places < fixed, places, moved)]].set(jnp.asarray(tallies, jnp.int32))

    tallies = jnp.where(number % 4 == 0, named(heavy_load, number // 4), named(ordinary, number - number // 4 - 1))
    mixed = jax.random.permutation(jax.random.fold_in(own, 3), amount)
    source_of, sink = mixed[0:amount // 2 * 2:2], mixed[1:amount // 2 * 2:2]
    margin = jnp.minimum(tallies[source_of] - 1, bound - tallies[sink]) // 2
    margin = jnp.where((source_of == order[0]) | (sink == order[0]) | (tallies[sink] == 0), 0, jnp.maximum(margin, 0))
    moved = jax.random.randint(jax.random.fold_in(own, 4), (amount // 2,), 0, 1 << 20) % (margin + 1)
    tallies = tallies.at[source_of].add(-moved).at[sink].add(moved)
    labels = jnp.searchsorted(jnp.cumsum(tallies), jnp.arange(rows * top), side="right").astype(jnp.int32)
    listing = labels.reshape(top, rows).T
    listing = listing[jax.random.permutation(jax.random.fold_in(own, 1), rows)]
    rotation = jax.random.randint(jax.random.fold_in(own, 2), (rows, 1), 0, top)
    return jnp.take_along_axis(listing, (jnp.arange(top)[None, :] + rotation) % top, axis=1)


def load_shares(number_of, total, bound, skew, full):
    loads = [(1 << 20) // math.isqrt(rank ** skew) + 1 for rank in range(1, number_of + 1)]
    largest = bound if full else min(bound, max(-(-total // number_of), total * loads[0] // sum(loads)))
    least = 1 if total - largest >= number_of - 1 else 0
    counts, surplus = [largest] + [least] * (number_of - 1), total - largest - least * (number_of - 1)
    while surplus > 0:
        movable = [i for i in range(1, number_of) if counts[i] < largest] or [i for i in range(1, number_of) if counts[i] < bound]
        mass, remaining = sum([loads[i] for i in movable]), surplus
        for i in movable:
            addition = min(bound - counts[i], max(1, remaining * loads[i] // mass), surplus)
            counts[i] = counts[i] + addition
            surplus = surplus - addition
    return np.array(counts)


def bell_draw(stream_key, dims, scale, most, shards=(), kind=jnp.bfloat16):
    level = steps_of(stream_key, dims, shards, -0.22, 0.18) if shards else 1.0
    array = jax.random.normal(stream_key, dims, jnp.float32) * scale * level
    return jnp.minimum(jnp.maximum(array, -most), most).astype(kind)


def setup_inputs(seed: int = 0) -> dict:
    key_list = jax.random.split(jax.random.key(seed), 13)
    text_embeds = draw_text_embeds(jax.random.fold_in(key_list[12], 71), 0)
    vision_tokens = bell_draw(key_list[1], (VTOK, D), 1.0, 6.0, ((0, 8), (1, 4)))
    vision_request_keys = jax.random.split(jax.random.fold_in(key_list[2], 1), VTOK // VT_GRP)
    vision_request_turns = jax.random.permutation(jax.random.fold_in(key_list[2], 3), VTOK // VT_GRP)
    vision_request = jax.vmap(lambda own, number: deal_out(jax.random.fold_in(key_list[2], 2), own, number, VT_GRP, REQUESTS, 1, CAP, 2))(vision_request_keys, vision_request_turns).reshape((VTOK, 1))
    image_start = with_ends(jax.random.randint(key_list[3], (REQUESTS,), 1, 17), jax.random.fold_in(key_list[3], 1), 1, 16).astype(jnp.int32)
    lengths = with_ends(jax.random.randint(key_list[4], (REQUESTS,), IMG_MAX + 17, SEQ_LEN + 1), jax.random.fold_in(key_list[4], 1), IMG_MAX + 17, SEQ_LEN).astype(jnp.int32)
    attn_gain = jnp.clip(1.0 + 0.1 * jax.random.normal(key_list[5], (D,), jnp.float32), 0.5, 1.5)
    w_query = draw_w_query(jax.random.fold_in(key_list[12], 71), 0)
    w_key = draw_w_key(jax.random.fold_in(key_list[12], 71), 0)
    w_value = bell_draw(key_list[8], (D, ATTN), D ** -0.5, 0.09375, ((0, 8), (1, 4)))
    w_out = bell_draw(key_list[9], (ATTN, D), ATTN ** -0.5, 0.125, ((1, 8),))
    final_gain = jnp.clip(1.0 + 0.15 * jax.random.normal(key_list[10], (D,), jnp.float32), 0.25, 1.75)
    lm_head = bell_draw(key_list[11], (D, VOCAB), (D // 9) ** -0.5, 0.25, ((1, 8),))
    return {"text_embeds": text_embeds, "vision_tokens": vision_tokens, "vision_request": vision_request, "image_start": image_start, "lengths": lengths, "attn_gain": attn_gain, "w_query": w_query, "w_key": w_key, "w_value": w_value, "w_out": w_out, "final_gain": final_gain, "lm_head": lm_head}


norm_epsilon = 1e-05

def reference(text_embeds, vision_tokens, vision_request, image_start, lengths, attn_gain, w_query, w_key, w_value, w_out, final_gain, lm_head):
    destination = vision_request[:, 0].astype(jnp.int32)
    onehot = (destination[:, None] == jnp.arange(REQUESTS, dtype=jnp.int32)[None, :]).astype(jnp.int32)
    ranking = lax.optimization_barrier(jnp.sum((jnp.cumsum(onehot, axis=0) - onehot) * onehot, axis=1)).astype(jnp.int32)
    positions = (destination * SEQ_LEN + jnp.take(image_start, destination) + ranking).astype(jnp.int32)
    states = text_embeds.at[positions].set(vision_tokens).reshape(REQUESTS, SEQ_LEN, D)

    def per_request(inputs):
        rows, length = inputs
        widened = rows.astype(jnp.float32)
        normed = (widened * lax.rsqrt(lax.optimization_barrier(jnp.mean(widened * widened, axis=1, keepdims=True)) + norm_epsilon) * attn_gain).astype(jnp.bfloat16)
        key_rows = jnp.dot(normed, w_key, preferred_element_type=jnp.float32).astype(jnp.bfloat16)
        value_rows = jnp.dot(normed, w_value, preferred_element_type=jnp.float32).astype(jnp.bfloat16)
        last_index = (length - 1).astype(jnp.int32)
        last_row = lax.dynamic_slice_in_dim(normed, last_index, 1, 0)
        query_row = jnp.dot(last_row, w_query, preferred_element_type=jnp.float32).astype(jnp.bfloat16)
        query_heads = query_row.reshape(HEADS, HD).astype(jnp.float32)
        key_heads = key_rows.reshape(SEQ_LEN, HEADS, HD).astype(jnp.float32)
        value_heads = value_rows.reshape(SEQ_LEN, HEADS, HD).astype(jnp.float32)
        scores = jnp.einsum('hc,jhc->hj', query_heads, key_heads) / math.sqrt(HD)
        live_keys = jnp.arange(SEQ_LEN, dtype=jnp.int32) < length
        scores = jnp.where(live_keys[None, :], scores, -jnp.inf)
        peak = lax.optimization_barrier(jnp.max(scores, axis=1, keepdims=True))
        shifted = jnp.exp(scores - peak)
        weights = (shifted / lax.optimization_barrier(jnp.sum(shifted, axis=1, keepdims=True))).astype(jnp.bfloat16)
        attended = jnp.einsum('hj,jhc->hc', weights.astype(jnp.float32), value_heads).astype(jnp.bfloat16)
        final_text = lax.dynamic_slice_in_dim(rows, last_index, 1, 0)[0]
        return (attended.reshape(HEADS * HD), final_text)
    attended, final_text = lax.map(per_request, (states, lengths))
    residual_out = final_text.astype(jnp.float32) + jnp.dot(attended, w_out, preferred_element_type=jnp.float32)
    mean_square = lax.optimization_barrier(jnp.mean(residual_out * residual_out, axis=1))
    scaled_out = (residual_out * final_gain).astype(jnp.bfloat16)
    logits = jnp.dot(scaled_out, lm_head, preferred_element_type=jnp.float32)
    max_logit = lax.optimization_barrier(jnp.max(logits * lax.rsqrt(mean_square + norm_epsilon)[:, None], axis=1))
    return (jnp.sqrt(mean_square), max_logit)
```

```python
import math

import jax
import jax.numpy as jnp
from jax import lax
from jax.sharding import PartitionSpec as P

HD = 128


norm_epsilon = 1e-05


def row_norm(rows, gain):
    widened = rows.astype(jnp.float32)
    return (
        widened
        * lax.rsqrt(jnp.mean(widened * widened, axis=1, keepdims=True) + norm_epsilon)
        * gain
    ).astype(jnp.bfloat16)


def pack_slots(tokens, destination, slot_index, groups, capacity):
    return (
        jnp.zeros((groups, capacity, tokens.shape[1]), jnp.bfloat16)
        .at[destination, slot_index]
        .set(tokens)
    )


def local(
    text_embeds,
    vision_tokens,
    vision_request,
    image_start,
    lengths,
    attn_gain,
    w_query,
    w_key,
    w_value,
    w_out,
    final_gain,
    lm_head,
):
    groups = lax.axis_size("fsdp")
    seq_count = lax.axis_size("seq")
    group_index = lax.axis_index("fsdp")
    seq_index = lax.axis_index("seq")
    seq_len = text_embeds.shape[0]
    width = text_embeds.shape[1]
    columns = w_key.shape[1]
    heads_local = columns // HD
    dpiece = width // groups
    fpiece = width // seq_count
    quarter = groups // seq_count
    capacity = max(2, 2 * vision_tokens.shape[0] // groups)
    last_index = lengths[0] - 1
    destination = vision_request[:, 0]
    onehot = (destination[:, None] == jnp.arange(groups, dtype=jnp.int32)[None, :]).astype(
        jnp.int32
    )
    slot_index = jnp.sum((jnp.cumsum(onehot, axis=0) - onehot) * onehot, axis=1)
    counts = jnp.sum(onehot, axis=0)
    outbox = pack_slots(vision_tokens, destination, slot_index, groups, capacity)
    final_text = lax.dynamic_slice_in_dim(text_embeds, last_index, 1, 0)
    last_row = row_norm(final_text, attn_gain)
    last_pieces = jnp.stack(
        [last_row.reshape(groups, dpiece), final_text.reshape(groups, dpiece)], axis=1
    )
    last_parts = lax.all_to_all(last_pieces, "fsdp", split_axis=0, concat_axis=0, tiled=True)
    received = lax.all_to_all(outbox, "fsdp", split_axis=0, concat_axis=0, tiled=True)
    arrived = lax.all_to_all(counts[:, None], "fsdp", split_axis=0, concat_axis=0, tiled=True)
    query = lax.psum(
        jnp.dot(last_parts[:, 0], w_query, preferred_element_type=jnp.float32), "fsdp"
    ).astype(jnp.bfloat16)
    gain_part = lax.dynamic_slice_in_dim(attn_gain, group_index * dpiece, dpiece, 0)
    probe_part = (
        jnp.einsum(
            "rhc,dhc->rhd",
            query.reshape(groups, heads_local, HD),
            w_key.reshape(dpiece, heads_local, HD),
            preferred_element_type=jnp.float32,
        )
        * gain_part
    ).astype(jnp.bfloat16)
    probe = lax.all_to_all(probe_part, "fsdp", split_axis=0, concat_axis=0, tiled=True)
    probe = probe.transpose(1, 0, 2).reshape(heads_local, width)
    probe = lax.all_to_all(probe, "seq", split_axis=1, concat_axis=0, tiled=True)
    occupied = (
        (jnp.arange(capacity, dtype=jnp.int32)[None, :] < arrived).astype(jnp.int32).reshape(-1)
    )
    ranking = jnp.cumsum(occupied) - occupied
    positions = jnp.where(occupied > 0, image_start[0] + ranking, seq_len)
    text_piece = lax.dynamic_slice_in_dim(text_embeds, seq_index * fpiece, fpiece, 1)
    states = text_piece.at[positions].set(received.reshape(-1, fpiece), mode="drop")
    widened = states.astype(jnp.float32)
    squares = jnp.sum(widened * widened, axis=1)
    partial_scores = jnp.einsum("hd,jd->hj", probe, states, preferred_element_type=jnp.float32)
    summed = lax.psum(jnp.concatenate([partial_scores, squares[None, :]], axis=0), "seq")
    inverse = lax.rsqrt(summed[-1:] / width + norm_epsilon)
    scores = summed[:-1] * inverse / math.sqrt(HD)
    live_keys = jnp.arange(seq_len, dtype=jnp.int32) < lengths[0]
    scores = jnp.where(live_keys[None, :], scores, -jnp.inf)
    peak = jnp.max(scores, axis=1, keepdims=True)
    shifted = jnp.exp(scores - peak)
    weights = shifted / jnp.sum(shifted, axis=1, keepdims=True)
    mixed = jnp.dot(
        (weights * inverse).astype(jnp.bfloat16), states, preferred_element_type=jnp.float32
    )
    mixed_gain = lax.dynamic_slice_in_dim(attn_gain, seq_index * fpiece, fpiece, 0)
    mixed = (mixed * mixed_gain).astype(jnp.bfloat16)
    mixed = lax.all_to_all(mixed, "seq", split_axis=0, concat_axis=1, tiled=True)
    mixed = mixed.reshape(heads_local, groups, dpiece).transpose(1, 0, 2)
    mixed = lax.all_to_all(mixed, "fsdp", split_axis=0, concat_axis=0, tiled=True)
    attended = lax.psum(
        jnp.einsum(
            "rhd,dhc->rhc",
            mixed,
            w_value.reshape(dpiece, heads_local, HD),
            preferred_element_type=jnp.float32,
        ).reshape(groups, columns),
        "fsdp",
    ).astype(jnp.bfloat16)
    out_rows = lax.dynamic_slice_in_dim(w_out, seq_index * columns, columns, 0)
    projected = lax.psum(jnp.dot(attended, out_rows, preferred_element_type=jnp.float32), "seq")
    residual_out = last_parts[:, 1].astype(jnp.float32) + projected
    residual_out = lax.dynamic_slice_in_dim(residual_out, seq_index * quarter, quarter, 0)
    final_part = lax.dynamic_slice_in_dim(final_gain, group_index * dpiece, dpiece, 0)
    scaled_out = (residual_out * final_part[None, :]).astype(jnp.bfloat16)
    square_part = jnp.sum(residual_out * residual_out, axis=1)
    full_scaled = lax.all_gather(scaled_out, "fsdp", axis=1, tiled=True)
    mean_square = lax.psum(square_part, "fsdp") / width
    logits = jnp.dot(full_scaled, lm_head, preferred_element_type=jnp.float32)
    local_max = jnp.max(logits, axis=1) * lax.rsqrt(mean_square + norm_epsilon)
    max_logit = lax.pmax(local_max, "fsdp")
    return (jnp.sqrt(mean_square), max_logit)


def solution(mesh):
    return jax.shard_map(
        local,
        mesh=mesh,
        in_specs=(
            P("fsdp", None),
            P("fsdp", "seq"),
            P("fsdp", None),
            P("fsdp"),
            P("fsdp"),
            P(),
            P("fsdp", "seq"),
            P("fsdp", "seq"),
            P("fsdp", "seq"),
            P(None, "fsdp"),
            P(),
            P(None, "fsdp"),
        ),
        out_specs=(P("seq"), P("seq")),
        check_vma=False,
    )
```

```python
import functools
import math

import jax
import jax.numpy as jnp
from jax import lax
from jax.experimental import pallas as pl
from jax.experimental.pallas import tpu as pltpu
from jax.sharding import PartitionSpec as P

HD = 128


norm_epsilon = 1e-05


def row_norm(rows, gain):
    widened = rows.astype(jnp.float32)
    return (
        widened
        * lax.rsqrt(jnp.mean(widened * widened, axis=1, keepdims=True) + norm_epsilon)
        * gain
    ).astype(jnp.bfloat16)


def pack_slots(tokens, destination, slot_index, groups, capacity):
    return (
        jnp.zeros((groups, capacity, tokens.shape[1]), jnp.bfloat16)
        .at[destination, slot_index]
        .set(tokens)
    )


def local(
    text_embeds,
    vision_tokens,
    vision_request,
    image_start,
    lengths,
    attn_gain,
    w_query,
    w_key,
    w_value,
    w_out,
    final_gain,
    lm_head,
):
    groups = lax.axis_size("fsdp")
    seq_count = lax.axis_size("seq")
    group_index = lax.axis_index("fsdp")
    seq_index = lax.axis_index("seq")
    seq_len = text_embeds.shape[0]
    width = text_embeds.shape[1]
    columns = w_key.shape[1]
    heads_local = columns // HD
    dpiece = width // groups
    fpiece = width // seq_count
    quarter = groups // seq_count
    capacity = max(2, 2 * vision_tokens.shape[0] // groups)
    last_index = lengths[0] - 1
    destination = vision_request[:, 0]
    onehot = (destination[:, None] == jnp.arange(groups, dtype=jnp.int32)[None, :]).astype(
        jnp.int32
    )
    slot_index = jnp.sum((jnp.cumsum(onehot, axis=0) - onehot) * onehot, axis=1)
    counts = jnp.sum(onehot, axis=0)
    outbox = pack_slots(vision_tokens, destination, slot_index, groups, capacity)
    final_text = lax.dynamic_slice_in_dim(text_embeds, last_index, 1, 0)
    last_row = row_norm(final_text, attn_gain)
    last_pieces = jnp.stack(
        [last_row.reshape(groups, dpiece), final_text.reshape(groups, dpiece)], axis=1
    )
    last_parts = lax.all_to_all(last_pieces, "fsdp", split_axis=0, concat_axis=0, tiled=True)
    received = lax.all_to_all(outbox, "fsdp", split_axis=0, concat_axis=0, tiled=True)
    arrived = lax.all_to_all(counts[:, None], "fsdp", split_axis=0, concat_axis=0, tiled=True)
    query = lax.psum(
        jnp.dot(last_parts[:, 0], w_query, preferred_element_type=jnp.float32), "fsdp"
    ).astype(jnp.bfloat16)
    gain_part = lax.dynamic_slice_in_dim(attn_gain, group_index * dpiece, dpiece, 0)
    probe_part = (
        jnp.einsum(
            "rhc,dhc->rhd",
            query.reshape(groups, heads_local, HD),
            w_key.reshape(dpiece, heads_local, HD),
            preferred_element_type=jnp.float32,
        )
        * gain_part
    ).astype(jnp.bfloat16)
    probe = lax.all_to_all(probe_part, "fsdp", split_axis=0, concat_axis=0, tiled=True)
    probe = probe.transpose(1, 0, 2).reshape(heads_local, width)
    probe = lax.all_to_all(probe, "seq", split_axis=1, concat_axis=0, tiled=True)
    occupied = (
        (jnp.arange(capacity, dtype=jnp.int32)[None, :] < arrived).astype(jnp.int32).reshape(-1)
    )
    ranking = jnp.cumsum(occupied) - occupied
    positions = jnp.where(occupied > 0, image_start[0] + ranking, seq_len)
    text_piece = lax.dynamic_slice_in_dim(text_embeds, seq_index * fpiece, fpiece, 1)
    states = text_piece.at[positions].set(received.reshape(-1, fpiece), mode="drop")
    widened = states.astype(jnp.float32)
    squares = jnp.sum(widened * widened, axis=1)
    partial_scores = jnp.einsum("hd,jd->hj", probe, states, preferred_element_type=jnp.float32)
    summed = lax.psum(jnp.concatenate([partial_scores, squares[None, :]], axis=0), "seq")
    inverse = lax.rsqrt(summed[-1:] / width + norm_epsilon)
    scores = summed[:-1] * inverse / math.sqrt(HD)
    live_keys = jnp.arange(seq_len, dtype=jnp.int32) < lengths[0]
    scores = jnp.where(live_keys[None, :], scores, -jnp.inf)
    peak = jnp.max(scores, axis=1, keepdims=True)
    shifted = jnp.exp(scores - peak)
    weights = shifted / jnp.sum(shifted, axis=1, keepdims=True)
    mixed = jnp.dot(
        (weights * inverse).astype(jnp.bfloat16), states, preferred_element_type=jnp.float32
    )
    mixed_gain = lax.dynamic_slice_in_dim(attn_gain, seq_index * fpiece, fpiece, 0)
    mixed = (mixed * mixed_gain).astype(jnp.bfloat16)
    mixed = lax.all_to_all(mixed, "seq", split_axis=0, concat_axis=1, tiled=True)
    mixed = mixed.reshape(heads_local, groups, dpiece).transpose(1, 0, 2)
    mixed = lax.all_to_all(mixed, "fsdp", split_axis=0, concat_axis=0, tiled=True)
    attended = lax.psum(
        jnp.einsum(
            "rhd,dhc->rhc",
            mixed,
            w_value.reshape(dpiece, heads_local, HD),
            preferred_element_type=jnp.float32,
        ).reshape(groups, columns),
        "fsdp",
    ).astype(jnp.bfloat16)
    out_rows = lax.dynamic_slice_in_dim(w_out, seq_index * columns, columns, 0)
    projected = lax.psum(jnp.dot(attended, out_rows, preferred_element_type=jnp.float32), "seq")
    residual_out = last_parts[:, 1].astype(jnp.float32) + projected
    residual_out = lax.dynamic_slice_in_dim(residual_out, seq_index * quarter, quarter, 0)
    final_part = lax.dynamic_slice_in_dim(final_gain, group_index * dpiece, dpiece, 0)
    scaled_out = (residual_out * final_part[None, :]).astype(jnp.bfloat16)
    square_part = jnp.sum(residual_out * residual_out, axis=1)
    full_scaled = lax.all_gather(scaled_out, "fsdp", axis=1, tiled=True)
    mean_square = lax.psum(square_part, "fsdp") / width
    logits = jnp.dot(full_scaled, lm_head, preferred_element_type=jnp.float32)
    local_max = jnp.max(logits, axis=1) * lax.rsqrt(mean_square + norm_epsilon)
    max_logit = lax.pmax(local_max, "fsdp")
    return (jnp.sqrt(mean_square), max_logit)


MESH = pl.DeviceIdType.MESH
F32 = jnp.float32
BF16 = jnp.bfloat16


def dot(a, b):
    return jnp.dot(a, b, preferred_element_type=F32)


def dot_rows(a, b):
    return lax.dot_general(a, b, (((1,), (1,)), ((), ())), preferred_element_type=F32)


def iota(shape, axis):
    return lax.broadcasted_iota(jnp.int32, shape, axis)


def fused_kernel(
    groups,
    seq_count,
    capacity,
    request,
    start,
    lengths,
    attn_gain,
    final_gain,
    text_hbm,
    vision_hbm,
    wq_hbm,
    wk_hbm,
    wv_hbm,
    wo_hbm,
    lm_hbm,
    rms_out,
    max_out,
    text,
    vision,
    wq,
    wk,
    wv,
    wo,
    lm,
    states,
    heads_in,
    last_send,
    last_recv,
    box_send,
    box_recv,
    count_send,
    count_recv,
    query_send,
    query_recv,
    key_send,
    key_recv,
    score_recv,
    mix_send,
    mix_recv,
    att_send,
    att_recv,
    out_recv,
    scaled_send,
    scaled_recv,
    logit_send,
    logit_recv,
    peak_recv,
    local_sem,
    send_sem,
    recv_sem,
):
    f = lax.axis_index("fsdp")
    s = lax.axis_index("seq")
    devices = groups * seq_count
    seq_len, width = text.shape
    rows_per = width // groups
    piece = width // seq_count
    owners = groups // seq_count
    columns = wq.shape[1]
    local_heads = columns // HD
    heads = local_heads * seq_count
    vtok = vision.shape[0]
    half = rows_per // 2

    barrier = pltpu.get_barrier_semaphore()
    me = f * seq_count + s

    def greet(k, carry):
        t = lax.rem(me + k, devices)
        pl.semaphore_signal(
            barrier,
            inc=1,
            device_id=(lax.div(t, seq_count), lax.rem(t, seq_count)),
            device_id_type=MESH,
        )
        return carry

    lax.fori_loop(1, devices, greet, 0)

    def fetch(index, source, target):
        copy = pltpu.make_async_copy(source, target, local_sem.at[index])
        copy.start()
        return copy

    get_text = fetch(0, text_hbm, text)
    get_vision = fetch(1, vision_hbm, vision)
    get_wq = fetch(2, wq_hbm, wq)
    get_wk = fetch(3, wk_hbm, wk)
    get_wv = fetch(4, wv_hbm, wv)
    get_wo = fetch(5, wo_hbm.at[pl.ds(pl.multiple_of(s * columns, columns), columns)], wo)
    get_lm = fetch(6, lm_hbm.at[pl.ds(pl.multiple_of(s * piece, piece), piece)], lm)

    sent = []

    def copy_of(phase, slot, from_slot, source, target, to_f, to_s):
        return pltpu.make_async_remote_copy(
            src_ref=source,
            dst_ref=target,
            send_sem=send_sem.at[phase, slot],
            recv_sem=recv_sem.at[phase, from_slot],
            device_id=(to_f, to_s),
            device_id_type=MESH,
        )

    def push(*what):
        copy = copy_of(*what)
        copy.start()
        sent.append(copy)

    def arrive(phase, slot, target):
        copy_of(phase, 0, slot, target, target, f, s).wait_recv()

    def across_groups(phase, source, target):
        for k in range(1, groups):
            t = lax.rem(f + k, groups)
            push(phase, k, f, source(t), target(f), t, s)

    def from_groups(phase, target):
        for k in range(1, groups):
            o = lax.rem(f + groups - k, groups)
            arrive(phase, o, target(o))

    def across_seq(phase, source, target):
        for k in range(1, seq_count):
            t = lax.rem(s + k, seq_count)
            push(phase, k, s, source(t), target(s), f, t)

    def from_seq(phase, target):
        for k in range(1, seq_count):
            o = lax.rem(s + seq_count - k, seq_count)
            arrive(phase, o, target(o))

    length = lengths[0]
    tail = (seq_len - 8) // 16 * 16
    get_text.wait()
    tail_rows = text[tail:, :].astype(F32)
    here = iota((seq_len - tail, 1), 0) == length - 1 - tail
    last = jnp.sum(jnp.where(here, tail_rows, 0.0), axis=0, keepdims=True)
    scale = lax.rsqrt(jnp.mean(last * last, axis=1, keepdims=True) + norm_epsilon)
    normed = (last * scale * attn_gain[...]).astype(BF16).astype(F32)
    for g in range(groups):
        span = slice(g * rows_per, (g + 1) * rows_per)
        last_send[g, 0:1, :] = normed[:, span]
        last_send[g, 1:2, :] = last[:, span]
    last_recv[f] = last_send[f]
    pl.semaphore_wait(barrier, devices - 1)
    across_groups(0, lambda t: last_send.at[t], lambda me_f: last_recv.at[me_f])

    named = request[...]
    member = jnp.where(iota((groups, vtok), 0) == named, 1.0, 0.0)
    earlier = jnp.where(iota((vtok, vtok), 0) < iota((vtok, vtok), 1), 1.0, 0.0)
    before = dot(member.astype(BF16), earlier.astype(BF16))
    rank = jnp.sum(before * member, axis=0, keepdims=True)
    counts = jnp.broadcast_to(jnp.sum(member, axis=1, keepdims=True), (groups, 128))
    for g in range(groups):
        count_send[g] = counts[g : g + 1, :]
    count_recv[f] = count_send[f]
    across_groups(1, lambda t: count_send.at[t], lambda me_f: count_recv.at[me_f])
    slot = named.astype(F32) * capacity + rank
    slots = groups * capacity
    pick = jnp.where(iota((slots, vtok), 0).astype(F32) == slot, 1.0, 0.0).astype(BF16)
    get_vision.wait()
    box_send[...] = dot(pick, vision[...]).astype(BF16).reshape(groups, capacity, piece)
    box_recv[f] = box_send[f]
    across_groups(2, lambda t: box_send.at[t], lambda me_f: box_recv.at[me_f])

    from_groups(0, lambda o: last_recv.at[o])
    get_wq.wait()
    query_part = dot(last_recv[:, 0, :].astype(BF16), wq[...])
    query_send[...] = query_part
    query_recv[f] = query_part
    across_groups(3, lambda t: query_send, lambda me_f: query_recv.at[me_f])
    get_wk.wait()
    from_groups(3, lambda o: query_recv.at[o])
    query = jnp.sum(query_recv[...], axis=0).astype(BF16)

    gain_rows = attn_gain[:, pl.ds(pl.multiple_of(f * rows_per, rows_per), rows_per)]
    for h in range(local_heads):
        span = slice(h * HD, (h + 1) * HD)
        key_send[:, h, :] = dot_rows(query[:, span], wk[:, span]) * gain_rows
    home = lax.div(f, owners)
    inner = lax.rem(f, owners)
    at_home = home == s
    own_key = copy_of(4, 0, inner * seq_count + s, key_send.at[f], key_recv.at[inner, s], f, home)

    @pl.when(at_home)
    def _():
        key_recv[inner, s] = key_send[f]

    @pl.when(jnp.logical_not(at_home))
    def _():
        own_key.start()

    for k in range(1, groups):
        t = lax.rem(f + k, groups)
        push(4, k, inner * seq_count + s, key_send.at[t], key_recv.at[inner, s], t, home)

    from_groups(1, lambda o: count_recv.at[o])
    tally = count_recv[:, 0, :]
    tallies = jnp.concatenate([tally] * (slots // 128), axis=1)
    source_of = iota((groups, slots), 0)
    owner = lax.div(iota((groups, slots), 1), capacity)
    arrived = jnp.sum(jnp.where(source_of == owner, tallies, 0.0), axis=0, keepdims=True)
    offset = jnp.sum(jnp.where(source_of < owner, tallies, 0.0), axis=0, keepdims=True)
    within = lax.rem(iota((1, slots), 1), capacity).astype(F32)
    first = start[0].astype(F32)
    position = jnp.where(within < arrived, first + offset + within, -1.0)
    place = jnp.where(iota((seq_len, slots), 0).astype(F32) == position, 1.0, 0.0).astype(BF16)
    total = jnp.sum(tally[:, :1], axis=0, keepdims=True)
    row = iota((seq_len, 1), 0).astype(F32)
    taken = jnp.logical_and(row >= first, row < first + total)
    from_groups(2, lambda o: box_recv.at[o])
    step = min(256, piece)
    ones = jnp.ones((8, step), BF16)
    squares = jnp.zeros((8, seq_len), F32)
    for c in range(piece // step):
        span = slice(c * step, (c + 1) * step)
        placed = dot(place, box_recv[:, :, span].reshape(slots, step))
        at = pl.multiple_of(s * piece + c * step, step)
        value = jnp.where(taken, placed, text[:, pl.ds(at, step)].astype(F32))
        states[:, span] = value.astype(BF16)
        square = value * value
        high = square.astype(BF16)
        low = (square - high.astype(F32)).astype(BF16)
        squares = squares + dot_rows(ones, high) + dot_rows(ones, low)

    for b in range(owners):
        for k in range(seq_count):
            o = lax.rem(s + k, seq_count)
            if k:
                arrive(4, b * seq_count + o, key_recv.at[b, o])
            else:

                @pl.when(jnp.logical_not(f == s * owners + b))
                def _(o=o, b=b):
                    arrive(4, b * seq_count + o, key_recv.at[b, o])

    for o in range(seq_count):
        for b in range(owners):
            heads_in[
                o * local_heads : (o + 1) * local_heads, b * rows_per : (b + 1) * rows_per
            ] = key_recv[b, o]
    part = dot_rows(heads_in[...].astype(BF16), states[...])
    score_recv[s, :heads] = part
    score_recv[s, heads:] = squares
    across_seq(5, lambda t: score_recv.at[s], lambda me_s: score_recv.at[me_s])
    from_seq(5, lambda o: score_recv.at[o])
    summed = jnp.sum(score_recv[...], axis=0)
    inverse = lax.rsqrt(summed[heads : heads + 1] / width + norm_epsilon)
    live = iota((1, seq_len), 1) < length
    scores = jnp.where(live, summed[:heads] * inverse / math.sqrt(HD), -jnp.inf)
    shifted = jnp.exp(scores - jnp.max(scores, axis=1, keepdims=True))
    weights = shifted / jnp.sum(shifted, axis=1, keepdims=True)
    mixed = dot((weights * inverse).astype(BF16), states[...])
    mixed = mixed * attn_gain[:, pl.ds(pl.multiple_of(s * piece, piece), piece)]

    for o in range(seq_count):
        for b in range(owners):
            mix_send[b, o] = mixed[
                o * local_heads : (o + 1) * local_heads, b * rows_per : (b + 1) * rows_per
            ]
    own_mix = []
    for b in range(owners):
        t = s * owners + b
        copy = copy_of(6, b * seq_count, f, mix_send.at[b, s], mix_recv.at[f], t, s)
        own_mix.append((t, copy))

        @pl.when(f == t)
        def _(b=b):
            mix_recv[f] = mix_send[b, s]

        @pl.when(jnp.logical_not(f == t))
        def _(copy=copy):
            copy.start()

        for k in range(1, seq_count):
            o = lax.rem(s + k, seq_count)
            push(6, b * seq_count + k, f, mix_send.at[b, o], mix_recv.at[f], t, o)
    get_wv.wait()
    from_groups(6, lambda o: mix_recv.at[o])

    @pl.when(jnp.logical_not(at_home))
    def _():
        arrive(6, f, mix_recv.at[f])

    for h in range(local_heads):
        span = slice(h * HD, (h + 1) * HD)
        att_send[:, span] = dot(mix_recv[:, h, :].astype(BF16), wv[:, span])
    att_recv[f] = att_send[...]
    across_groups(7, lambda t: att_send, lambda me_f: att_recv.at[me_f])
    get_wo.wait()
    from_groups(7, lambda o: att_recv.at[o])
    attended = jnp.sum(att_recv[...], axis=0).astype(BF16)

    out_recv[s] = dot(attended, wo[...])
    across_seq(8, lambda t: out_recv.at[s], lambda me_s: out_recv.at[me_s])
    from_seq(8, lambda o: out_recv.at[o])
    residual = last_recv[:, 1, :] + jnp.sum(out_recv[...], axis=0)
    square_part = jnp.sum(residual * residual, axis=1, keepdims=True)
    final_rows = final_gain[:, pl.ds(pl.multiple_of(f * rows_per, rows_per), rows_per)]
    scaled = residual * final_rows
    scaled_send[...] = jnp.concatenate([scaled[:, :half], scaled[:, half:]], axis=0).astype(BF16)

    scaled_out = [
        copy_of(
            9,
            k,
            inner,
            scaled_send,
            scaled_recv.at[inner],
            lax.rem(f + k, groups),
            s,
        )
        for k in range(1, groups)
    ]

    @pl.when(at_home)
    def _():
        scaled_recv[inner] = scaled_send[...]
        for copy in scaled_out:
            copy.start()

    get_lm.wait()
    for b in range(owners):

        @pl.when(jnp.logical_not(f == s * owners + b))
        def _(b=b):
            arrive(9, b, scaled_recv.at[b])

    logits = jnp.zeros((groups, lm.shape[1]), F32)
    for b in range(owners):
        for c in range(2):
            at = b * rows_per + c * half
            logits = logits + dot(
                scaled_recv[b, c * groups : (c + 1) * groups, :], lm[at : at + half, :]
            )
    for o in range(seq_count):
        logit_send[o] = logits[o * owners : (o + 1) * owners]
    logit_recv[s] = logit_send[s]
    across_seq(10, lambda t: logit_send.at[t], lambda me_s: logit_recv.at[me_s])
    from_seq(10, lambda o: logit_recv.at[o])
    top = jnp.max(jnp.sum(logit_recv[...], axis=0), axis=1, keepdims=True)
    mine = iota((owners, groups), 1) - s * owners == iota((owners, groups), 0)
    squares_row = jnp.sum(
        jnp.where(iota((groups, groups), 0) == iota((groups, groups), 1), square_part, 0.0),
        axis=0,
        keepdims=True,
    )
    square_mine = jnp.sum(jnp.where(mine, squares_row, 0.0), axis=1, keepdims=True)
    lane = iota((owners, 128), 1)
    peak_recv[f] = jnp.where(lane < 64, top, square_mine)
    across_groups(11, lambda t: peak_recv.at[f], lambda me_f: peak_recv.at[me_f])
    from_groups(11, lambda o: peak_recv.at[o])
    everyone = peak_recv[...]
    best = jnp.max(everyone, axis=0)[:, :1]
    mean_square = jnp.sum(everyone, axis=0)[:, 64:65] / width
    rms_out[...] = jnp.broadcast_to(jnp.sqrt(mean_square), (owners, 128))
    max_out[...] = jnp.broadcast_to(best * lax.rsqrt(mean_square + norm_epsilon), (owners, 128))

    for copy in sent:
        copy.wait_send()

    @pl.when(jnp.logical_not(at_home))
    def _():
        own_key.wait_send()

    for t, copy in own_mix:

        @pl.when(jnp.logical_not(f == t))
        def _(copy=copy):
            copy.wait_send()

    @pl.when(at_home)
    def _():
        for copy in scaled_out:
            copy.wait_send()


def fused(
    text_embeds,
    vision_tokens,
    vision_request,
    image_start,
    lengths,
    attn_gain,
    w_query,
    w_key,
    w_value,
    w_out,
    final_gain,
    lm_head,
):
    groups = lax.axis_size("fsdp")
    seq_count = lax.axis_size("seq")
    seq_len, width = text_embeds.shape
    vtok, piece = vision_tokens.shape
    rows_per, columns = w_query.shape
    vocab = lm_head.shape[1]
    owners = groups // seq_count
    local_heads = columns // HD
    heads = local_heads * seq_count
    capacity = 2 * vtok // groups
    vmem = pl.BlockSpec(memory_space=pltpu.VMEM)
    smem = pl.BlockSpec(memory_space=pltpu.SMEM)
    any_space = pl.BlockSpec(memory_space=pl.ANY)
    phases = 12
    links = max(groups, owners * seq_count)
    rms, best = pl.pallas_call(
        functools.partial(fused_kernel, groups, seq_count, capacity),
        out_shape=[jax.ShapeDtypeStruct((owners, 128), F32)] * 2,
        in_specs=[vmem, smem, smem, vmem, vmem] + [any_space] * 7,
        out_specs=[vmem, vmem],
        scratch_shapes=[
            pltpu.VMEM((seq_len, width), BF16),
            pltpu.VMEM((vtok, piece), BF16),
            pltpu.VMEM((rows_per, columns), BF16),
            pltpu.VMEM((rows_per, columns), BF16),
            pltpu.VMEM((rows_per, columns), BF16),
            pltpu.VMEM((columns, rows_per), BF16),
            pltpu.VMEM((piece, vocab), BF16),
            pltpu.VMEM((seq_len, piece), BF16),
            pltpu.VMEM((heads, piece), F32),
            pltpu.VMEM((groups, 2, rows_per), F32),
            pltpu.VMEM((groups, 2, rows_per), F32),
            pltpu.VMEM((groups, capacity, piece), BF16),
            pltpu.VMEM((groups, capacity, piece), BF16),
            pltpu.VMEM((groups, 1, 128), F32),
            pltpu.VMEM((groups, 1, 128), F32),
            pltpu.VMEM((groups, columns), F32),
            pltpu.VMEM((groups, groups, columns), F32),
            pltpu.VMEM((groups, local_heads, rows_per), F32),
            pltpu.VMEM((owners, seq_count, local_heads, rows_per), F32),
            pltpu.VMEM((seq_count, heads + 8, seq_len), F32),
            pltpu.VMEM((owners, seq_count, local_heads, rows_per), F32),
            pltpu.VMEM((groups, local_heads, rows_per), F32),
            pltpu.VMEM((groups, columns), F32),
            pltpu.VMEM((groups, groups, columns), F32),
            pltpu.VMEM((seq_count, groups, rows_per), F32),
            pltpu.VMEM((2 * groups, rows_per // 2), BF16),
            pltpu.VMEM((owners, 2 * groups, rows_per // 2), BF16),
            pltpu.VMEM((seq_count, owners, vocab), F32),
            pltpu.VMEM((seq_count, owners, vocab), F32),
            pltpu.VMEM((groups, owners, 128), F32),
            pltpu.SemaphoreType.DMA((7,)),
            pltpu.SemaphoreType.DMA((phases, links)),
            pltpu.SemaphoreType.DMA((phases, links)),
        ],
        compiler_params=pltpu.CompilerParams(
            collective_id=0, has_side_effects=True, vmem_limit_bytes=48 * 2**20
        ),
        name="fused",
    )(
        vision_request.reshape(1, vtok),
        image_start,
        lengths,
        attn_gain.reshape(1, width),
        final_gain.reshape(1, width),
        text_embeds,
        vision_tokens,
        w_query,
        w_key,
        w_value,
        w_out,
        lm_head,
    )
    return rms[:, 0], best[:, 0]


def fits(mesh):
    groups, seq_count = mesh.shape["fsdp"], mesh.shape["seq"]
    return groups == 8 and groups % seq_count == 0


def solution(mesh):
    return jax.shard_map(
        fused if fits(mesh) else local,
        mesh=mesh,
        in_specs=(
            P("fsdp", None),
            P("fsdp", "seq"),
            P("fsdp", None),
            P("fsdp"),
            P("fsdp"),
            P(),
            P("fsdp", "seq"),
            P("fsdp", "seq"),
            P("fsdp", "seq"),
            P(None, "fsdp"),
            P(),
            P(None, "fsdp"),
        ),
        out_specs=(P("seq"), P("seq")),
        check_vma=False,
    )
```

```python
import functools
import math

import jax
import jax.numpy as jnp
from jax import lax
from jax.experimental import pallas as pl
from jax.experimental.pallas import tpu as pltpu
from jax.sharding import PartitionSpec as P

HD = 128


norm_epsilon = 1e-05


def row_norm(rows, gain):
    widened = rows.astype(jnp.float32)
    return (
        widened
        * lax.rsqrt(jnp.mean(widened * widened, axis=1, keepdims=True) + norm_epsilon)
        * gain
    ).astype(jnp.bfloat16)


def pack_slots(tokens, destination, slot_index, groups, capacity):
    return (
        jnp.zeros((groups, capacity, tokens.shape[1]), jnp.bfloat16)
        .at[destination, slot_index]
        .set(tokens)
    )


def local(
    text_embeds,
    vision_tokens,
    vision_request,
    image_start,
    lengths,
    attn_gain,
    w_query,
    w_key,
    w_value,
    w_out,
    final_gain,
    lm_head,
):
    groups = lax.axis_size("fsdp")
    seq_count = lax.axis_size("seq")
    group_index = lax.axis_index("fsdp")
    seq_index = lax.axis_index("seq")
    seq_len = text_embeds.shape[0]
    width = text_embeds.shape[1]
    columns = w_key.shape[1]
    heads_local = columns // HD
    dpiece = width // groups
    fpiece = width // seq_count
    quarter = groups // seq_count
    capacity = max(2, 2 * vision_tokens.shape[0] // groups)
    last_index = lengths[0] - 1
    destination = vision_request[:, 0]
    onehot = (destination[:, None] == jnp.arange(groups, dtype=jnp.int32)[None, :]).astype(
        jnp.int32
    )
    slot_index = jnp.sum((jnp.cumsum(onehot, axis=0) - onehot) * onehot, axis=1)
    counts = jnp.sum(onehot, axis=0)
    outbox = pack_slots(vision_tokens, destination, slot_index, groups, capacity)
    final_text = lax.dynamic_slice_in_dim(text_embeds, last_index, 1, 0)
    last_row = row_norm(final_text, attn_gain)
    last_pieces = jnp.stack(
        [last_row.reshape(groups, dpiece), final_text.reshape(groups, dpiece)], axis=1
    )
    last_parts = lax.all_to_all(last_pieces, "fsdp", split_axis=0, concat_axis=0, tiled=True)
    received = lax.all_to_all(outbox, "fsdp", split_axis=0, concat_axis=0, tiled=True)
    arrived = lax.all_to_all(counts[:, None], "fsdp", split_axis=0, concat_axis=0, tiled=True)
    query = lax.psum(
        jnp.dot(last_parts[:, 0], w_query, preferred_element_type=jnp.float32), "fsdp"
    ).astype(jnp.bfloat16)
    gain_part = lax.dynamic_slice_in_dim(attn_gain, group_index * dpiece, dpiece, 0)
    probe_part = (
        jnp.einsum(
            "rhc,dhc->rhd",
            query.reshape(groups, heads_local, HD),
            w_key.reshape(dpiece, heads_local, HD),
            preferred_element_type=jnp.float32,
        )
        * gain_part
    ).astype(jnp.bfloat16)
    probe = lax.all_to_all(probe_part, "fsdp", split_axis=0, concat_axis=0, tiled=True)
    probe = probe.transpose(1, 0, 2).reshape(heads_local, width)
    probe = lax.all_to_all(probe, "seq", split_axis=1, concat_axis=0, tiled=True)
    occupied = (
        (jnp.arange(capacity, dtype=jnp.int32)[None, :] < arrived).astype(jnp.int32).reshape(-1)
    )
    ranking = jnp.cumsum(occupied) - occupied
    positions = jnp.where(occupied > 0, image_start[0] + ranking, seq_len)
    text_piece = lax.dynamic_slice_in_dim(text_embeds, seq_index * fpiece, fpiece, 1)
    states = text_piece.at[positions].set(received.reshape(-1, fpiece), mode="drop")
    widened = states.astype(jnp.float32)
    squares = jnp.sum(widened * widened, axis=1)
    partial_scores = jnp.einsum("hd,jd->hj", probe, states, preferred_element_type=jnp.float32)
    summed = lax.psum(jnp.concatenate([partial_scores, squares[None, :]], axis=0), "seq")
    inverse = lax.rsqrt(summed[-1:] / width + norm_epsilon)
    scores = summed[:-1] * inverse / math.sqrt(HD)
    live_keys = jnp.arange(seq_len, dtype=jnp.int32) < lengths[0]
    scores = jnp.where(live_keys[None, :], scores, -jnp.inf)
    peak = jnp.max(scores, axis=1, keepdims=True)
    shifted = jnp.exp(scores - peak)
    weights = shifted / jnp.sum(shifted, axis=1, keepdims=True)
    mixed = jnp.dot(
        (weights * inverse).astype(jnp.bfloat16), states, preferred_element_type=jnp.float32
    )
    mixed_gain = lax.dynamic_slice_in_dim(attn_gain, seq_index * fpiece, fpiece, 0)
    mixed = (mixed * mixed_gain).astype(jnp.bfloat16)
    mixed = lax.all_to_all(mixed, "seq", split_axis=0, concat_axis=1, tiled=True)
    mixed = mixed.reshape(heads_local, groups, dpiece).transpose(1, 0, 2)
    mixed = lax.all_to_all(mixed, "fsdp", split_axis=0, concat_axis=0, tiled=True)
    attended = lax.psum(
        jnp.einsum(
            "rhd,dhc->rhc",
            mixed,
            w_value.reshape(dpiece, heads_local, HD),
            preferred_element_type=jnp.float32,
        ).reshape(groups, columns),
        "fsdp",
    ).astype(jnp.bfloat16)
    out_rows = lax.dynamic_slice_in_dim(w_out, seq_index * columns, columns, 0)
    projected = lax.psum(jnp.dot(attended, out_rows, preferred_element_type=jnp.float32), "seq")
    residual_out = last_parts[:, 1].astype(jnp.float32) + projected
    residual_out = lax.dynamic_slice_in_dim(residual_out, seq_index * quarter, quarter, 0)
    final_part = lax.dynamic_slice_in_dim(final_gain, group_index * dpiece, dpiece, 0)
    scaled_out = (residual_out * final_part[None, :]).astype(jnp.bfloat16)
    square_part = jnp.sum(residual_out * residual_out, axis=1)
    full_scaled = lax.all_gather(scaled_out, "fsdp", axis=1, tiled=True)
    mean_square = lax.psum(square_part, "fsdp") / width
    logits = jnp.dot(full_scaled, lm_head, preferred_element_type=jnp.float32)
    local_max = jnp.max(logits, axis=1) * lax.rsqrt(mean_square + norm_epsilon)
    max_logit = lax.pmax(local_max, "fsdp")
    return (jnp.sqrt(mean_square), max_logit)


MESH = pl.DeviceIdType.MESH
F32 = jnp.float32
BF16 = jnp.bfloat16


def dot(a, b):
    return jnp.dot(a, b, preferred_element_type=F32)


def dot_rows(a, b):
    return lax.dot_general(a, b, (((1,), (1,)), ((), ())), preferred_element_type=F32)


def iota(shape, axis):
    return lax.broadcasted_iota(jnp.int32, shape, axis)


def folded(rows):
    half = rows.shape[1] // 2
    return jnp.concatenate([rows[:, :half], rows[:, half:]], axis=0).astype(BF16)


def unfolded(rows):
    half = rows.shape[0] // 2
    return jnp.concatenate([rows[:half], rows[half:]], axis=1)


def fused_kernel(
    groups,
    seq_count,
    capacity,
    request,
    start,
    lengths,
    attn_gain,
    final_gain,
    text_hbm,
    vision_hbm,
    wq_hbm,
    wk_hbm,
    wv_hbm,
    wo_hbm,
    lm_hbm,
    rms_out,
    max_out,
    text,
    vision,
    wq,
    wk,
    wv,
    wo,
    lm,
    states,
    heads_in,
    last_send,
    last_recv,
    box_send,
    box_recv,
    count_send,
    count_recv,
    query_send,
    query_recv,
    key_send,
    key_recv,
    score_recv,
    square_recv,
    mix_send,
    mix_recv,
    att_send,
    att_recv,
    out_recv,
    scaled_send,
    scaled_recv,
    peak_send,
    peak_recv,
    local_sem,
    send_sem,
    recv_sem,
):
    f = lax.axis_index("fsdp")
    s = lax.axis_index("seq")
    devices = groups * seq_count
    seq_len, width = text.shape
    rows_per = width // groups
    piece = width // seq_count
    owners = groups // seq_count
    columns = wq.shape[1]
    local_heads = columns // HD
    heads = local_heads * seq_count
    vtok = vision.shape[0]
    half = rows_per // 2

    barrier = pltpu.get_barrier_semaphore()
    me = f * seq_count + s

    def greet(k, carry):
        t = lax.rem(me + k, devices)
        pl.semaphore_signal(
            barrier,
            inc=1,
            device_id=(lax.div(t, seq_count), lax.rem(t, seq_count)),
            device_id_type=MESH,
        )
        return carry

    lax.fori_loop(1, devices, greet, 0)

    def fetch(index, source, target):
        copy = pltpu.make_async_copy(source, target, local_sem.at[index])
        copy.start()
        return copy

    get_text = fetch(0, text_hbm, text)
    get_vision = fetch(1, vision_hbm, vision)
    get_wq = fetch(2, wq_hbm, wq)
    get_wk = fetch(3, wk_hbm, wk)
    get_wv = fetch(4, wv_hbm, wv)
    get_wo = fetch(5, wo_hbm.at[pl.ds(pl.multiple_of(s * columns, columns), columns)], wo)
    words = lm.shape[0]
    vocab = lm_hbm.shape[0]
    final_seq = s == seq_count - 1
    final_words = vocab - (seq_count - 1) * words
    get_lm = pltpu.make_async_copy(
        lm_hbm.at[pl.ds(pl.multiple_of(s * words, words), words)], lm, local_sem.at[6]
    )
    get_lm_final = pltpu.make_async_copy(
        lm_hbm.at[vocab - final_words :], lm.at[:final_words], local_sem.at[6]
    )

    @pl.when(jnp.logical_not(final_seq))
    def _():
        get_lm.start()

    @pl.when(final_seq)
    def _():
        get_lm_final.start()
        if final_words < words:
            lm[final_words:, :] = jnp.zeros((words - final_words, width), BF16)

    sent = []

    def copy_of(phase, slot, from_slot, source, target, to_f, to_s):
        return pltpu.make_async_remote_copy(
            src_ref=source,
            dst_ref=target,
            send_sem=send_sem.at[phase, slot],
            recv_sem=recv_sem.at[phase, from_slot],
            device_id=(to_f, to_s),
            device_id_type=MESH,
        )

    def push(*what):
        copy = copy_of(*what)
        copy.start()
        sent.append(copy)

    def arrive(phase, slot, target):
        copy_of(phase, 0, slot, target, target, f, s).wait_recv()

    def across_groups(phase, source, target):
        for k in range(1, groups):
            t = lax.rem(f + k, groups)
            push(phase, k, f, source(t), target(f), t, s)

    def from_groups(phase, target):
        for k in range(1, groups):
            o = lax.rem(f + groups - k, groups)
            arrive(phase, o, target(o))

    def across_seq(phase, source, target):
        for k in range(1, seq_count):
            t = lax.rem(s + k, seq_count)
            push(phase, k, s, source(t), target(s), f, t)

    def from_seq(phase, target):
        for k in range(1, seq_count):
            o = lax.rem(s + seq_count - k, seq_count)
            arrive(phase, o, target(o))

    length = lengths[0]
    tail = (seq_len - 8) // 16 * 16
    get_text.wait()
    tail_rows = text[tail:, :].astype(F32)
    here = iota((seq_len - tail, 1), 0) == length - 1 - tail
    last = jnp.sum(jnp.where(here, tail_rows, 0.0), axis=0, keepdims=True)
    scale = lax.rsqrt(jnp.mean(last * last, axis=1, keepdims=True) + norm_epsilon)
    normed = (last * scale * attn_gain[...]).astype(BF16).astype(F32)
    for g in range(groups):
        span = slice(g * rows_per, (g + 1) * rows_per)
        last_send[g, 0:1, :] = normed[:, span]
        last_send[g, 1:2, :] = last[:, span]
    last_recv[f] = last_send[f]
    pl.semaphore_wait(barrier, devices - 1)
    across_groups(0, lambda t: last_send.at[t], lambda me_f: last_recv.at[me_f])

    named = request[...]
    member = jnp.where(iota((groups, vtok), 0) == named, 1.0, 0.0)
    earlier = jnp.where(iota((vtok, vtok), 0) < iota((vtok, vtok), 1), 1.0, 0.0)
    before = dot(member.astype(BF16), earlier.astype(BF16))
    rank = jnp.sum(before * member, axis=0, keepdims=True)
    counts = jnp.broadcast_to(jnp.sum(member, axis=1, keepdims=True), (groups, 128))
    for g in range(groups):
        count_send[g] = counts[g : g + 1, :]
    count_recv[f] = count_send[f]
    across_groups(1, lambda t: count_send.at[t], lambda me_f: count_recv.at[me_f])
    slot = named.astype(F32) * capacity + rank
    slots = groups * capacity
    pick = jnp.where(iota((slots, vtok), 0).astype(F32) == slot, 1.0, 0.0).astype(BF16)
    get_vision.wait()
    box_send[...] = dot(pick, vision[...]).astype(BF16).reshape(groups, capacity, piece)
    box_recv[f] = box_send[f]
    across_groups(2, lambda t: box_send.at[t], lambda me_f: box_recv.at[me_f])

    from_groups(0, lambda o: last_recv.at[o])
    get_wq.wait()
    query_part = dot(last_recv[:, 0, :].astype(BF16), wq[...])
    query_send[...] = folded(query_part)
    query_recv[f] = query_send[...]
    across_groups(3, lambda t: query_send, lambda me_f: query_recv.at[me_f])
    get_wk.wait()
    from_groups(3, lambda o: query_recv.at[o])
    query = unfolded(jnp.sum(query_recv[...].astype(F32), axis=0)).astype(BF16)

    gain_rows = attn_gain[:, pl.ds(pl.multiple_of(f * rows_per, rows_per), rows_per)]
    for h in range(local_heads):
        span = slice(h * HD, (h + 1) * HD)
        key_send[:, h, :] = dot_rows(query[:, span], wk[:, span]) * gain_rows
    home = lax.div(f, owners)
    inner = lax.rem(f, owners)
    at_home = home == s
    own_key = copy_of(4, 0, inner * seq_count + s, key_send.at[f], key_recv.at[inner, s], f, home)

    @pl.when(at_home)
    def _():
        key_recv[inner, s] = key_send[f]

    @pl.when(jnp.logical_not(at_home))
    def _():
        own_key.start()

    for k in range(1, groups):
        t = lax.rem(f + k, groups)
        push(4, k, inner * seq_count + s, key_send.at[t], key_recv.at[inner, s], t, home)

    from_groups(1, lambda o: count_recv.at[o])
    tally = count_recv[:, 0, :]
    tallies = jnp.concatenate([tally] * (slots // 128), axis=1)
    source_of = iota((groups, slots), 0)
    owner = lax.div(iota((groups, slots), 1), capacity)
    arrived = jnp.sum(jnp.where(source_of == owner, tallies, 0.0), axis=0, keepdims=True)
    offset = jnp.sum(jnp.where(source_of < owner, tallies, 0.0), axis=0, keepdims=True)
    within = lax.rem(iota((1, slots), 1), capacity).astype(F32)
    first = start[0].astype(F32)
    position = jnp.where(within < arrived, first + offset + within, -1.0)
    place = jnp.where(iota((seq_len, slots), 0).astype(F32) == position, 1.0, 0.0).astype(BF16)
    total = jnp.sum(tally[:, :1], axis=0, keepdims=True)
    row = iota((seq_len, 1), 0).astype(F32)
    taken = jnp.logical_and(row >= first, row < first + total)
    from_groups(2, lambda o: box_recv.at[o])
    step = min(256, piece)
    ones = jnp.ones((8, step), BF16)
    squares = jnp.zeros((8, seq_len), F32)
    for c in range(piece // step):
        span = slice(c * step, (c + 1) * step)
        placed = dot(place, box_recv[:, :, span].reshape(slots, step))
        at = pl.multiple_of(s * piece + c * step, step)
        value = jnp.where(taken, placed, text[:, pl.ds(at, step)].astype(F32))
        states[:, span] = value.astype(BF16)
        square = value * value
        high = square.astype(BF16)
        low = (square - high.astype(F32)).astype(BF16)
        squares = squares + dot_rows(ones, high) + dot_rows(ones, low)

    square_recv[s] = squares
    across_seq(11, lambda t: square_recv.at[s], lambda me_s: square_recv.at[me_s])
    for b in range(owners):
        for k in range(seq_count):
            o = lax.rem(s + k, seq_count)
            if k:
                arrive(4, b * seq_count + o, key_recv.at[b, o])
            else:

                @pl.when(jnp.logical_not(f == s * owners + b))
                def _(o=o, b=b):
                    arrive(4, b * seq_count + o, key_recv.at[b, o])

    for o in range(seq_count):
        for b in range(owners):
            heads_in[
                o * local_heads : (o + 1) * local_heads, b * rows_per : (b + 1) * rows_per
            ] = key_recv[b, o]
    part = dot_rows(heads_in[...].astype(BF16), states[...])
    score_recv[s] = part
    across_seq(5, lambda t: score_recv.at[s], lambda me_s: score_recv.at[me_s])
    from_seq(5, lambda o: score_recv.at[o])
    from_seq(11, lambda o: square_recv.at[o])
    square_sums = jnp.sum(square_recv[...], axis=0)
    inverse = lax.rsqrt(square_sums[:1] / width + norm_epsilon)
    summed = jnp.sum(score_recv[...], axis=0)
    live = iota((1, seq_len), 1) < length
    scores = jnp.where(live, summed * inverse / math.sqrt(HD), -jnp.inf)
    shifted = jnp.exp(scores - jnp.max(scores, axis=1, keepdims=True))
    weights = shifted / jnp.sum(shifted, axis=1, keepdims=True)
    mixed = dot((weights * inverse).astype(BF16), states[...])
    mixed = mixed * attn_gain[:, pl.ds(pl.multiple_of(s * piece, piece), piece)]

    for o in range(seq_count):
        for b in range(owners):
            mix_send[b, o] = mixed[
                o * local_heads : (o + 1) * local_heads, b * rows_per : (b + 1) * rows_per
            ]
    own_mix = []
    for b in range(owners):
        t = s * owners + b
        copy = copy_of(6, b * seq_count, f, mix_send.at[b, s], mix_recv.at[f], t, s)
        own_mix.append((t, copy))

        @pl.when(f == t)
        def _(b=b):
            mix_recv[f] = mix_send[b, s]

        @pl.when(jnp.logical_not(f == t))
        def _(copy=copy):
            copy.start()

        for k in range(1, seq_count):
            o = lax.rem(s + k, seq_count)
            push(6, b * seq_count + k, f, mix_send.at[b, o], mix_recv.at[f], t, o)
    get_wv.wait()
    from_groups(6, lambda o: mix_recv.at[o])

    @pl.when(jnp.logical_not(at_home))
    def _():
        arrive(6, f, mix_recv.at[f])

    att_part = [
        dot(mix_recv[:, h, :].astype(BF16), wv[:, h * HD : (h + 1) * HD])
        for h in range(local_heads)
    ]
    att_send[...] = folded(jnp.concatenate(att_part, axis=1))
    att_recv[f] = att_send[...]
    across_groups(7, lambda t: att_send, lambda me_f: att_recv.at[me_f])
    get_wo.wait()
    from_groups(7, lambda o: att_recv.at[o])
    attended = unfolded(jnp.sum(att_recv[...].astype(F32), axis=0)).astype(BF16)

    out_recv[s] = dot(attended, wo[...])
    across_seq(8, lambda t: out_recv.at[s], lambda me_s: out_recv.at[me_s])
    from_seq(8, lambda o: out_recv.at[o])
    residual = last_recv[:, 1, :] + jnp.sum(out_recv[...], axis=0)
    square_part = jnp.sum(residual * residual, axis=1, keepdims=True)
    final_rows = final_gain[:, pl.ds(pl.multiple_of(f * rows_per, rows_per), rows_per)]
    scaled = residual * final_rows
    scaled_send[...] = folded(scaled)

    scaled_recv[f] = scaled_send[...]
    across_groups(9, lambda t: scaled_send, lambda me_f: scaled_recv.at[me_f])

    @pl.when(jnp.logical_not(final_seq))
    def _():
        get_lm.wait()

    @pl.when(final_seq)
    def _():
        get_lm_final.wait()

    logits = jnp.zeros((groups, words), F32)
    for k in range(groups):
        o = lax.rem(f + groups - k, groups)
        if k:
            arrive(9, o, scaled_recv.at[o])
        for c in range(2):
            at = pl.multiple_of(o * rows_per + c * half, half)
            logits = logits + dot_rows(
                scaled_recv[o, c * groups : (c + 1) * groups, :], lm[:, pl.ds(at, half)]
            )
    word = iota((1, words), 1) + s * words
    top = jnp.max(jnp.where(word < vocab, logits, -jnp.inf), axis=1, keepdims=True)
    peaks = jnp.where(iota((groups, 128), 1) < 64, top, square_part)
    for o in range(seq_count):
        peak_send[o] = peaks[o * owners : (o + 1) * owners]
    peak_recv[me] = peak_send[s]
    for k in range(1, devices):
        t = lax.rem(me + k, devices)
        t_f, t_s = lax.div(t, seq_count), lax.rem(t, seq_count)
        push(10, k, me, peak_send.at[t_s], peak_recv.at[me], t_f, t_s)
    for k in range(1, devices):
        o = lax.rem(me + devices - k, devices)
        arrive(10, o, peak_recv.at[o])
    everyone = peak_recv[...]
    best = jnp.max(everyone, axis=0)[:, :1]
    mean_square = jnp.sum(everyone, axis=0)[:, 64:65] / (width * seq_count)
    rms_out[...] = jnp.broadcast_to(jnp.sqrt(mean_square), (owners, 128))
    max_out[...] = jnp.broadcast_to(best * lax.rsqrt(mean_square + norm_epsilon), (owners, 128))

    for copy in sent:
        copy.wait_send()

    @pl.when(jnp.logical_not(at_home))
    def _():
        own_key.wait_send()

    for t, copy in own_mix:

        @pl.when(jnp.logical_not(f == t))
        def _(copy=copy):
            copy.wait_send()


def fused(
    text_embeds,
    vision_tokens,
    vision_request,
    image_start,
    lengths,
    attn_gain,
    w_query,
    w_key,
    w_value,
    w_out,
    final_gain,
    lm_head,
):
    groups = lax.axis_size("fsdp")
    seq_count = lax.axis_size("seq")
    seq_len, width = text_embeds.shape
    vtok, piece = vision_tokens.shape
    rows_per, columns = w_query.shape
    words = -(-lm_head.shape[1] // (16 * seq_count)) * 16
    owners = groups // seq_count
    local_heads = columns // HD
    heads = local_heads * seq_count
    capacity = 2 * vtok // groups
    vmem = pl.BlockSpec(memory_space=pltpu.VMEM)
    smem = pl.BlockSpec(memory_space=pltpu.SMEM)
    any_space = pl.BlockSpec(memory_space=pl.ANY)
    phases = 12
    links = groups * seq_count
    rms, best = pl.pallas_call(
        functools.partial(fused_kernel, groups, seq_count, capacity),
        out_shape=[jax.ShapeDtypeStruct((owners, 128), F32)] * 2,
        in_specs=[vmem, smem, smem, vmem, vmem] + [any_space] * 7,
        out_specs=[vmem, vmem],
        scratch_shapes=[
            pltpu.VMEM((seq_len, width), BF16),
            pltpu.VMEM((vtok, piece), BF16),
            pltpu.VMEM((rows_per, columns), BF16),
            pltpu.VMEM((rows_per, columns), BF16),
            pltpu.VMEM((rows_per, columns), BF16),
            pltpu.VMEM((columns, rows_per), BF16),
            pltpu.VMEM((words, width), BF16),
            pltpu.VMEM((seq_len, piece), BF16),
            pltpu.VMEM((heads, piece), F32),
            pltpu.VMEM((groups, 2, rows_per), F32),
            pltpu.VMEM((groups, 2, rows_per), F32),
            pltpu.VMEM((groups, capacity, piece), BF16),
            pltpu.VMEM((groups, capacity, piece), BF16),
            pltpu.VMEM((groups, 1, 128), F32),
            pltpu.VMEM((groups, 1, 128), F32),
            pltpu.VMEM((2 * groups, columns // 2), BF16),
            pltpu.VMEM((groups, 2 * groups, columns // 2), BF16),
            pltpu.VMEM((groups, local_heads, rows_per), F32),
            pltpu.VMEM((owners, seq_count, local_heads, rows_per), F32),
            pltpu.VMEM((seq_count, heads, seq_len), F32),
            pltpu.VMEM((seq_count, 8, seq_len), F32),
            pltpu.VMEM((owners, seq_count, local_heads, rows_per), F32),
            pltpu.VMEM((groups, local_heads, rows_per), F32),
            pltpu.VMEM((2 * groups, columns // 2), BF16),
            pltpu.VMEM((groups, 2 * groups, columns // 2), BF16),
            pltpu.VMEM((seq_count, groups, rows_per), F32),
            pltpu.VMEM((2 * groups, rows_per // 2), BF16),
            pltpu.VMEM((groups, 2 * groups, rows_per // 2), BF16),
            pltpu.VMEM((seq_count, owners, 128), F32),
            pltpu.VMEM((groups * seq_count, owners, 128), F32),
            pltpu.SemaphoreType.DMA((7,)),
            pltpu.SemaphoreType.DMA((phases, links)),
            pltpu.SemaphoreType.DMA((phases, links)),
        ],
        compiler_params=pltpu.CompilerParams(
            collective_id=0, has_side_effects=True, vmem_limit_bytes=56 * 2**20
        ),
        name="fused",
    )(
        vision_request.reshape(1, vtok),
        image_start,
        lengths,
        attn_gain.reshape(1, width),
        final_gain.reshape(1, width),
        text_embeds,
        vision_tokens,
        w_query,
        w_key,
        w_value,
        w_out,
        lm_head.T,
    )
    return rms[:, 0], best[:, 0]


def fits(mesh):
    groups, seq_count = mesh.shape["fsdp"], mesh.shape["seq"]
    return groups == 8 and groups % seq_count == 0


def solution(mesh):
    return jax.shard_map(
        fused if fits(mesh) else local,
        mesh=mesh,
        in_specs=(
            P("fsdp", None),
            P("fsdp", "seq"),
            P("fsdp", None),
            P("fsdp"),
            P("fsdp"),
            P(),
            P("fsdp", "seq"),
            P("fsdp", "seq"),
            P("fsdp", "seq"),
            P(None, "fsdp"),
            P(),
            P(None, "fsdp"),
        ),
        out_specs=(P("seq"), P("seq")),
        check_vma=False,
    )
```

```python
import functools
import math

import jax
import jax.numpy as jnp
from jax import lax
from jax.experimental import pallas as pl
from jax.experimental.pallas import tpu as pltpu
from jax.sharding import PartitionSpec as P

HD = 128


norm_epsilon = 1e-05


def row_norm(rows, gain):
    widened = rows.astype(jnp.float32)
    return (
        widened
        * lax.rsqrt(jnp.mean(widened * widened, axis=1, keepdims=True) + norm_epsilon)
        * gain
    ).astype(jnp.bfloat16)


def pack_slots(tokens, destination, slot_index, groups, capacity):
    return (
        jnp.zeros((groups, capacity, tokens.shape[1]), jnp.bfloat16)
        .at[destination, slot_index]
        .set(tokens)
    )


def local(
    text_embeds,
    vision_tokens,
    vision_request,
    image_start,
    lengths,
    attn_gain,
    w_query,
    w_key,
    w_value,
    w_out,
    final_gain,
    lm_head,
):
    groups = lax.axis_size("fsdp")
    seq_count = lax.axis_size("seq")
    group_index = lax.axis_index("fsdp")
    seq_index = lax.axis_index("seq")
    seq_len = text_embeds.shape[0]
    width = text_embeds.shape[1]
    columns = w_key.shape[1]
    heads_local = columns // HD
    dpiece = width // groups
    fpiece = width // seq_count
    quarter = groups // seq_count
    capacity = max(2, 2 * vision_tokens.shape[0] // groups)
    last_index = lengths[0] - 1
    destination = vision_request[:, 0]
    onehot = (destination[:, None] == jnp.arange(groups, dtype=jnp.int32)[None, :]).astype(
        jnp.int32
    )
    slot_index = jnp.sum((jnp.cumsum(onehot, axis=0) - onehot) * onehot, axis=1)
    counts = jnp.sum(onehot, axis=0)
    outbox = pack_slots(vision_tokens, destination, slot_index, groups, capacity)
    final_text = lax.dynamic_slice_in_dim(text_embeds, last_index, 1, 0)
    last_row = row_norm(final_text, attn_gain)
    last_pieces = jnp.stack(
        [last_row.reshape(groups, dpiece), final_text.reshape(groups, dpiece)], axis=1
    )
    last_parts = lax.all_to_all(last_pieces, "fsdp", split_axis=0, concat_axis=0, tiled=True)
    received = lax.all_to_all(outbox, "fsdp", split_axis=0, concat_axis=0, tiled=True)
    arrived = lax.all_to_all(counts[:, None], "fsdp", split_axis=0, concat_axis=0, tiled=True)
    query = lax.psum(
        jnp.dot(last_parts[:, 0], w_query, preferred_element_type=jnp.float32), "fsdp"
    ).astype(jnp.bfloat16)
    gain_part = lax.dynamic_slice_in_dim(attn_gain, group_index * dpiece, dpiece, 0)
    probe_part = (
        jnp.einsum(
            "rhc,dhc->rhd",
            query.reshape(groups, heads_local, HD),
            w_key.reshape(dpiece, heads_local, HD),
            preferred_element_type=jnp.float32,
        )
        * gain_part
    ).astype(jnp.bfloat16)
    probe = lax.all_to_all(probe_part, "fsdp", split_axis=0, concat_axis=0, tiled=True)
    probe = probe.transpose(1, 0, 2).reshape(heads_local, width)
    probe = lax.all_to_all(probe, "seq", split_axis=1, concat_axis=0, tiled=True)
    occupied = (
        (jnp.arange(capacity, dtype=jnp.int32)[None, :] < arrived).astype(jnp.int32).reshape(-1)
    )
    ranking = jnp.cumsum(occupied) - occupied
    positions = jnp.where(occupied > 0, image_start[0] + ranking, seq_len)
    text_piece = lax.dynamic_slice_in_dim(text_embeds, seq_index * fpiece, fpiece, 1)
    states = text_piece.at[positions].set(received.reshape(-1, fpiece), mode="drop")
    widened = states.astype(jnp.float32)
    squares = jnp.sum(widened * widened, axis=1)
    partial_scores = jnp.einsum("hd,jd->hj", probe, states, preferred_element_type=jnp.float32)
    summed = lax.psum(jnp.concatenate([partial_scores, squares[None, :]], axis=0), "seq")
    inverse = lax.rsqrt(summed[-1:] / width + norm_epsilon)
    scores = summed[:-1] * inverse / math.sqrt(HD)
    live_keys = jnp.arange(seq_len, dtype=jnp.int32) < lengths[0]
    scores = jnp.where(live_keys[None, :], scores, -jnp.inf)
    peak = jnp.max(scores, axis=1, keepdims=True)
    shifted = jnp.exp(scores - peak)
    weights = shifted / jnp.sum(shifted, axis=1, keepdims=True)
    mixed = jnp.dot(
        (weights * inverse).astype(jnp.bfloat16), states, preferred_element_type=jnp.float32
    )
    mixed_gain = lax.dynamic_slice_in_dim(attn_gain, seq_index * fpiece, fpiece, 0)
    mixed = (mixed * mixed_gain).astype(jnp.bfloat16)
    mixed = lax.all_to_all(mixed, "seq", split_axis=0, concat_axis=1, tiled=True)
    mixed = mixed.reshape(heads_local, groups, dpiece).transpose(1, 0, 2)
    mixed = lax.all_to_all(mixed, "fsdp", split_axis=0, concat_axis=0, tiled=True)
    attended = lax.psum(
        jnp.einsum(
            "rhd,dhc->rhc",
            mixed,
            w_value.reshape(dpiece, heads_local, HD),
            preferred_element_type=jnp.float32,
        ).reshape(groups, columns),
        "fsdp",
    ).astype(jnp.bfloat16)
    out_rows = lax.dynamic_slice_in_dim(w_out, seq_index * columns, columns, 0)
    projected = lax.psum(jnp.dot(attended, out_rows, preferred_element_type=jnp.float32), "seq")
    residual_out = last_parts[:, 1].astype(jnp.float32) + projected
    residual_out = lax.dynamic_slice_in_dim(residual_out, seq_index * quarter, quarter, 0)
    final_part = lax.dynamic_slice_in_dim(final_gain, group_index * dpiece, dpiece, 0)
    scaled_out = (residual_out * final_part[None, :]).astype(jnp.bfloat16)
    square_part = jnp.sum(residual_out * residual_out, axis=1)
    full_scaled = lax.all_gather(scaled_out, "fsdp", axis=1, tiled=True)
    mean_square = lax.psum(square_part, "fsdp") / width
    logits = jnp.dot(full_scaled, lm_head, preferred_element_type=jnp.float32)
    local_max = jnp.max(logits, axis=1) * lax.rsqrt(mean_square + norm_epsilon)
    max_logit = lax.pmax(local_max, "fsdp")
    return (jnp.sqrt(mean_square), max_logit)


MESH = pl.DeviceIdType.MESH
F32 = jnp.float32
BF16 = jnp.bfloat16


def dot(a, b):
    return jnp.dot(a, b, preferred_element_type=F32)


def dot_rows(a, b):
    return lax.dot_general(a, b, (((1,), (1,)), ((), ())), preferred_element_type=F32)


def iota(shape, axis):
    return lax.broadcasted_iota(jnp.int32, shape, axis)


def folded(rows):
    half = rows.shape[1] // 2
    return jnp.concatenate([rows[:, :half], rows[:, half:]], axis=0).astype(BF16)


def unfolded(rows):
    half = rows.shape[0] // 2
    return jnp.concatenate([rows[:half], rows[half:]], axis=1)


def wrap(index, size):
    return jnp.where(index >= size, index - size, index)


def fused_kernel(
    groups,
    seq_count,
    capacity,
    request,
    start,
    lengths,
    attn_gain,
    final_gain,
    text_hbm,
    vision_hbm,
    wq_hbm,
    wk_hbm,
    wv_hbm,
    wo_hbm,
    lm_hbm,
    rms_out,
    max_out,
    text,
    vision,
    wq,
    wk,
    wv,
    wo,
    lm,
    states,
    heads_in,
    last_send,
    last_recv,
    box_send,
    box_recv,
    query_send,
    query_recv,
    key_send,
    key_recv,
    score_recv,
    mix_send,
    mix_recv,
    att_send,
    att_recv,
    out_recv,
    scaled_send,
    scaled_recv,
    peak_send,
    peak_recv,
    local_sem,
    send_sem,
    recv_sem,
):
    f = lax.axis_index("fsdp")
    s = lax.axis_index("seq")
    devices = groups * seq_count
    seq_len, width = text.shape
    rows_per = width // groups
    piece = width // seq_count
    owners = groups // seq_count
    columns = wq.shape[1]
    local_heads = columns // HD
    heads = local_heads * seq_count
    vtok = vision.shape[0]
    half = rows_per // 2

    barrier = pltpu.get_barrier_semaphore()
    me = f * seq_count + s

    others = []
    for k in range(groups):
        for j in range(seq_count):
            if k or j:
                others.append((wrap(f + k, groups), wrap(s + j, seq_count)))
    for other in others:
        pl.semaphore_signal(barrier, inc=1, device_id=other, device_id_type=MESH)

    def fetch(index, source, target):
        copy = pltpu.make_async_copy(source, target, local_sem.at[index])
        copy.start()
        return copy

    get_text = fetch(0, text_hbm, text)

    sent = []

    def copy_of(phase, slot, from_slot, source, target, to_f, to_s):
        return pltpu.make_async_remote_copy(
            src_ref=source,
            dst_ref=target,
            send_sem=send_sem.at[phase, slot],
            recv_sem=recv_sem.at[phase, from_slot],
            device_id=(to_f, to_s),
            device_id_type=MESH,
        )

    def push(*what):
        copy = copy_of(*what)
        copy.start()
        sent.append(copy)

    def arrive(phase, slot, target):
        copy_of(phase, 0, slot, target, target, f, s).wait_recv()

    def across_groups(phase, source, target, offsets=None):
        for k in offsets or range(1, groups):
            t = wrap(f + k, groups)
            push(phase, k, f, source(t), target(f), t, s)

    def from_groups(phase, target):
        for k in range(1, groups):
            o = wrap(f + groups - k, groups)
            arrive(phase, o, target(o))

    def across_seq(phase, source, target):
        for k in range(1, seq_count):
            t = wrap(s + k, seq_count)
            push(phase, k, s, source(t), target(s), f, t)

    def from_seq(phase, target):
        for k in range(1, seq_count):
            o = wrap(s + seq_count - k, seq_count)
            arrive(phase, o, target(o))

    length = lengths[0]
    tail = (seq_len - 8) // 16 * 16
    get_text.wait()
    get_vision = fetch(1, vision_hbm, vision)
    get_wq = fetch(2, wq_hbm, wq)
    get_wk = fetch(3, wk_hbm, wk)
    get_wv = fetch(4, wv_hbm, wv)
    get_wo = fetch(5, wo_hbm.at[pl.ds(pl.multiple_of(s * columns, columns), columns)], wo)
    words = lm.shape[0]
    vocab = lm_hbm.shape[0]
    final_seq = s == seq_count - 1
    final_words = vocab - (seq_count - 1) * words
    get_lm = pltpu.make_async_copy(
        lm_hbm.at[pl.ds(pl.multiple_of(s * words, words), words)], lm, local_sem.at[6]
    )
    get_lm_final = pltpu.make_async_copy(
        lm_hbm.at[vocab - final_words :], lm.at[:final_words], local_sem.at[6]
    )

    @pl.when(jnp.logical_not(final_seq))
    def _():
        get_lm.start()

    @pl.when(final_seq)
    def _():
        get_lm_final.start()
        if final_words < words:
            lm[final_words:, :] = jnp.zeros((words - final_words, width), BF16)

    tail_rows = text[tail:, :].astype(F32)
    here = iota((seq_len - tail, 1), 0) == length - 1 - tail
    last = jnp.sum(jnp.where(here, tail_rows, 0.0), axis=0, keepdims=True)
    scale = lax.rsqrt(jnp.mean(last * last, axis=1, keepdims=True) + norm_epsilon)
    normed = (last * scale * attn_gain[...]).astype(BF16).astype(F32)
    named = request[...]
    member = jnp.where(iota((groups, vtok), 0) == named, 1.0, 0.0)
    counts = jnp.broadcast_to(jnp.sum(member, axis=1, keepdims=True), (groups, rows_per))
    for g in range(groups):
        span = slice(g * rows_per, (g + 1) * rows_per)
        last_send[g, 0:1, :] = normed[:, span]
        last_send[g, 1:2, :] = last[:, span]
        last_send[g, 2:3, :] = counts[g : g + 1, :]
    last_recv[f] = last_send[f]
    pl.semaphore_wait(barrier, devices - 1)
    across_groups(0, lambda t: last_send.at[t], lambda me_f: last_recv.at[me_f])

    earlier = jnp.where(iota((vtok, vtok), 0) < iota((vtok, vtok), 1), 1.0, 0.0)
    before = dot(member.astype(BF16), earlier.astype(BF16))
    rank = jnp.sum(before * member, axis=0, keepdims=True)
    slot = named.astype(F32) * capacity + rank
    slots = groups * capacity
    pick = jnp.where(iota((slots, vtok), 0).astype(F32) == slot, 1.0, 0.0).astype(BF16)
    get_vision.wait()
    box_send[...] = dot(pick, vision[...]).astype(BF16).reshape(groups, capacity, piece)
    box_recv[f] = box_send[f]
    order = [groups // 2] + [k for k in range(1, groups) if k != groups // 2]
    early, late = order[: groups // 2], order[groups // 2 :]
    across_groups(2, lambda t: box_send.at[t], lambda me_f: box_recv.at[me_f], early)

    from_groups(0, lambda o: last_recv.at[o])
    get_wq.wait()
    query_part = dot(last_recv[:, 0, :].astype(BF16), wq[...])
    query_send[...] = folded(query_part)
    query_recv[f] = query_send[...]
    across_groups(3, lambda t: query_send, lambda me_f: query_recv.at[me_f])
    across_groups(2, lambda t: box_send.at[t], lambda me_f: box_recv.at[me_f], late)
    get_wk.wait()
    from_groups(3, lambda o: query_recv.at[o])
    query = unfolded(jnp.sum(query_recv[...].astype(F32), axis=0)).astype(BF16)

    gain_rows = attn_gain[:, pl.ds(pl.multiple_of(f * rows_per, rows_per), rows_per)]
    for h in range(local_heads):
        span = slice(h * HD, (h + 1) * HD)
        key_send[:, h, :] = dot_rows(query[:, span], wk[:, span]) * gain_rows
    home = lax.div(f, owners)
    inner = lax.rem(f, owners)
    at_home = home == s
    own_key = copy_of(4, 0, inner * seq_count + s, key_send.at[f], key_recv.at[inner, s], f, home)

    @pl.when(at_home)
    def _():
        key_recv[inner, s] = key_send[f]

    @pl.when(jnp.logical_not(at_home))
    def _():
        own_key.start()

    for k in range(1, groups):
        t = wrap(f + k, groups)
        push(4, k, inner * seq_count + s, key_send.at[t], key_recv.at[inner, s], t, home)

    tally = last_recv[:, 2, :128]
    tallies = jnp.concatenate([tally] * (slots // 128), axis=1)
    source_of = iota((groups, slots), 0)
    owner = lax.div(iota((groups, slots), 1), capacity)
    arrived = jnp.sum(jnp.where(source_of == owner, tallies, 0.0), axis=0, keepdims=True)
    offset = jnp.sum(jnp.where(source_of < owner, tallies, 0.0), axis=0, keepdims=True)
    within = lax.rem(iota((1, slots), 1), capacity).astype(F32)
    first = start[0].astype(F32)
    position = jnp.where(within < arrived, first + offset + within, -1.0)
    place = jnp.where(iota((seq_len, slots), 0).astype(F32) == position, 1.0, 0.0).astype(BF16)
    total = jnp.sum(tally[:, :1], axis=0, keepdims=True)
    row = iota((seq_len, 1), 0).astype(F32)
    taken = jnp.logical_and(row >= first, row < first + total)
    from_groups(2, lambda o: box_recv.at[o])
    step = min(256, piece)
    squares = jnp.zeros((seq_len, 1), F32)
    for c in range(piece // step):
        span = slice(c * step, (c + 1) * step)
        placed = dot(place, box_recv[:, :, span].reshape(slots, step))
        at = pl.multiple_of(s * piece + c * step, step)
        value = jnp.where(taken, placed, text[:, pl.ds(at, step)].astype(F32))
        states[:, span] = value.astype(BF16)
        squares = squares + jnp.sum(value * value, axis=1, keepdims=True)

    for b in range(owners):
        for k in range(seq_count):
            o = wrap(s + k, seq_count)
            if k:
                arrive(4, b * seq_count + o, key_recv.at[b, o])
            else:

                @pl.when(jnp.logical_not(f == s * owners + b))
                def _(o=o, b=b):
                    arrive(4, b * seq_count + o, key_recv.at[b, o])

    for o in range(seq_count):
        for b in range(owners):
            heads_in[
                o * local_heads : (o + 1) * local_heads, b * rows_per : (b + 1) * rows_per
            ] = key_recv[b, o]
    heads_in[heads:, :] = jnp.zeros((8, piece), F32)
    part = dot_rows(states[...], heads_in[...].astype(BF16))
    part = jnp.where(iota((1, heads + 8), 1) == heads, squares, part)
    score_recv[s] = part.T
    across_seq(5, lambda t: score_recv.at[s], lambda me_s: score_recv.at[me_s])
    from_seq(5, lambda o: score_recv.at[o])
    summed = jnp.sum(score_recv[...], axis=0)
    inverse = lax.rsqrt(summed[heads : heads + 1] / width + norm_epsilon)
    live = iota((1, seq_len), 1) < length
    scores = jnp.where(live, summed[:heads] * inverse / math.sqrt(HD), -jnp.inf)
    shifted = jnp.exp(scores - jnp.max(scores, axis=1, keepdims=True))
    weights = shifted / jnp.sum(shifted, axis=1, keepdims=True)
    mixed = dot((weights * inverse).astype(BF16), states[...])
    mixed = mixed * attn_gain[:, pl.ds(pl.multiple_of(s * piece, piece), piece)]

    for o in range(seq_count):
        for b in range(owners):
            mix_send[b, o] = mixed[
                o * local_heads : (o + 1) * local_heads, b * rows_per : (b + 1) * rows_per
            ]
    own_mix = []
    for b in range(owners):
        t = s * owners + b
        copy = copy_of(6, b * seq_count, f, mix_send.at[b, s], mix_recv.at[f], t, s)
        own_mix.append((t, copy))

        @pl.when(f == t)
        def _(b=b):
            mix_recv[f] = mix_send[b, s]

        @pl.when(jnp.logical_not(f == t))
        def _(copy=copy):
            copy.start()

        for k in range(1, seq_count):
            o = wrap(s + k, seq_count)
            push(6, b * seq_count + k, f, mix_send.at[b, o], mix_recv.at[f], t, o)
    get_wv.wait()
    from_groups(6, lambda o: mix_recv.at[o])

    @pl.when(jnp.logical_not(at_home))
    def _():
        arrive(6, f, mix_recv.at[f])

    att_part = [
        dot(mix_recv[:, h, :].astype(BF16), wv[:, h * HD : (h + 1) * HD])
        for h in range(local_heads)
    ]
    att_send[...] = folded(jnp.concatenate(att_part, axis=1))
    att_recv[f] = att_send[...]
    across_groups(7, lambda t: att_send, lambda me_f: att_recv.at[me_f])
    get_wo.wait()
    from_groups(7, lambda o: att_recv.at[o])
    attended = unfolded(jnp.sum(att_recv[...].astype(F32), axis=0)).astype(BF16)

    out_recv[s] = dot(attended, wo[...])
    across_seq(8, lambda t: out_recv.at[s], lambda me_s: out_recv.at[me_s])
    from_seq(8, lambda o: out_recv.at[o])
    residual = last_recv[:, 1, :] + jnp.sum(out_recv[...], axis=0)
    square_part = jnp.sum(residual * residual, axis=1, keepdims=True)
    final_rows = final_gain[:, pl.ds(pl.multiple_of(f * rows_per, rows_per), rows_per)]
    scaled = residual * final_rows
    scaled_send[...] = folded(scaled)

    scaled_recv[f] = scaled_send[...]
    across_groups(9, lambda t: scaled_send, lambda me_f: scaled_recv.at[me_f])

    @pl.when(jnp.logical_not(final_seq))
    def _():
        get_lm.wait()

    @pl.when(final_seq)
    def _():
        get_lm_final.wait()

    from_groups(9, lambda o: scaled_recv.at[o])
    scaled_full = jnp.concatenate([unfolded(scaled_recv[o]) for o in range(groups)], axis=1)
    logits = dot_rows(lm[...], scaled_full)
    word = iota((words, 1), 0) + s * words
    top = jnp.max(jnp.where(word < vocab, logits, -jnp.inf), axis=0, keepdims=True)
    diagonal = iota((groups, groups), 0) == iota((groups, groups), 1)
    top = jnp.max(jnp.where(diagonal, top, -jnp.inf), axis=1, keepdims=True)
    peaks = jnp.where(iota((groups, 128), 1) < 64, top, square_part)
    for o in range(seq_count):
        peak_send[o] = peaks[o * owners : (o + 1) * owners]
    peak_recv[me] = peak_send[s]
    for k, (t_f, t_s) in enumerate(others):
        push(10, k, me, peak_send.at[t_s], peak_recv.at[me], t_f, t_s)
    for t_f, t_s in others:
        o = t_f * seq_count + t_s
        arrive(10, o, peak_recv.at[o])
    everyone = peak_recv[...]
    best = jnp.max(everyone, axis=0)[:, :1]
    mean_square = jnp.sum(everyone, axis=0)[:, 64:65] / (width * seq_count)
    rms_out[...] = jnp.broadcast_to(jnp.sqrt(mean_square), (owners, 128))
    max_out[...] = jnp.broadcast_to(best * lax.rsqrt(mean_square + norm_epsilon), (owners, 128))

    for copy in sent:
        copy.wait_send()

    @pl.when(jnp.logical_not(at_home))
    def _():
        own_key.wait_send()

    for t, copy in own_mix:

        @pl.when(jnp.logical_not(f == t))
        def _(copy=copy):
            copy.wait_send()


def fused(
    text_embeds,
    vision_tokens,
    vision_request,
    image_start,
    lengths,
    attn_gain,
    w_query,
    w_key,
    w_value,
    w_out,
    final_gain,
    lm_head,
):
    groups = lax.axis_size("fsdp")
    seq_count = lax.axis_size("seq")
    seq_len, width = text_embeds.shape
    vtok, piece = vision_tokens.shape
    rows_per, columns = w_query.shape
    words = -(-lm_head.shape[1] // (16 * seq_count)) * 16
    owners = groups // seq_count
    local_heads = columns // HD
    heads = local_heads * seq_count
    capacity = 2 * vtok // groups
    vmem = pl.BlockSpec(memory_space=pltpu.VMEM)
    smem = pl.BlockSpec(memory_space=pltpu.SMEM)
    any_space = pl.BlockSpec(memory_space=pl.ANY)
    phases = 12
    links = groups * seq_count
    rms, best = pl.pallas_call(
        functools.partial(fused_kernel, groups, seq_count, capacity),
        out_shape=[jax.ShapeDtypeStruct((owners, 128), F32)] * 2,
        in_specs=[vmem, smem, smem, vmem, vmem] + [any_space] * 7,
        out_specs=[vmem, vmem],
        scratch_shapes=[
            pltpu.VMEM((seq_len, width), BF16),
            pltpu.VMEM((vtok, piece), BF16),
            pltpu.VMEM((rows_per, columns), BF16),
            pltpu.VMEM((rows_per, columns), BF16),
            pltpu.VMEM((rows_per, columns), BF16),
            pltpu.VMEM((columns, rows_per), BF16),
            pltpu.VMEM((words, width), BF16),
            pltpu.VMEM((seq_len, piece), BF16),
            pltpu.VMEM((heads + 8, piece), F32),
            pltpu.VMEM((groups, 3, rows_per), F32),
            pltpu.VMEM((groups, 3, rows_per), F32),
            pltpu.VMEM((groups, capacity, piece), BF16),
            pltpu.VMEM((groups, capacity, piece), BF16),
            pltpu.VMEM((2 * groups, columns // 2), BF16),
            pltpu.VMEM((groups, 2 * groups, columns // 2), BF16),
            pltpu.VMEM((groups, local_heads, rows_per), F32),
            pltpu.VMEM((owners, seq_count, local_heads, rows_per), F32),
            pltpu.VMEM((seq_count, heads + 8, seq_len), F32),
            pltpu.VMEM((owners, seq_count, local_heads, rows_per), F32),
            pltpu.VMEM((groups, local_heads, rows_per), F32),
            pltpu.VMEM((2 * groups, columns // 2), BF16),
            pltpu.VMEM((groups, 2 * groups, columns // 2), BF16),
            pltpu.VMEM((seq_count, groups, rows_per), F32),
            pltpu.VMEM((2 * groups, rows_per // 2), BF16),
            pltpu.VMEM((groups, 2 * groups, rows_per // 2), BF16),
            pltpu.VMEM((seq_count, owners, 128), F32),
            pltpu.VMEM((groups * seq_count, owners, 128), F32),
            pltpu.SemaphoreType.DMA((7,)),
            pltpu.SemaphoreType.DMA((phases, links)),
            pltpu.SemaphoreType.DMA((phases, links)),
        ],
        compiler_params=pltpu.CompilerParams(
            collective_id=0, has_side_effects=True, vmem_limit_bytes=56 * 2**20
        ),
        name="fused",
    )(
        vision_request.reshape(1, vtok),
        image_start,
        lengths,
        attn_gain.reshape(1, width),
        final_gain.reshape(1, width),
        text_embeds,
        vision_tokens,
        w_query,
        w_key,
        w_value,
        w_out,
        lm_head.T,
    )
    return rms[:, 0], best[:, 0]


def fits(mesh):
    groups, seq_count = mesh.shape["fsdp"], mesh.shape["seq"]
    return groups == 8 and groups % seq_count == 0


def solution(mesh):
    return jax.shard_map(
        fused if fits(mesh) else local,
        mesh=mesh,
        in_specs=(
            P("fsdp", None),
            P("fsdp", "seq"),
            P("fsdp", None),
            P("fsdp"),
            P("fsdp"),
            P(),
            P("fsdp", "seq"),
            P("fsdp", "seq"),
            P("fsdp", "seq"),
            P(None, "fsdp"),
            P(),
            P(None, "fsdp"),
        ),
        out_specs=(P("seq"), P("seq")),
        check_vma=False,
    )
```

```python
import functools
import math

import jax
import jax.numpy as jnp
from jax import lax
from jax.experimental import pallas as pl
from jax.experimental.pallas import tpu as pltpu
from jax.sharding import PartitionSpec as P

HD = 128


norm_epsilon = 1e-05


def row_norm(rows, gain):
    widened = rows.astype(jnp.float32)
    return (
        widened
        * lax.rsqrt(jnp.mean(widened * widened, axis=1, keepdims=True) + norm_epsilon)
        * gain
    ).astype(jnp.bfloat16)


def pack_slots(tokens, destination, slot_index, groups, capacity):
    return (
        jnp.zeros((groups, capacity, tokens.shape[1]), jnp.bfloat16)
        .at[destination, slot_index]
        .set(tokens)
    )


def local(
    text_embeds,
    vision_tokens,
    vision_request,
    image_start,
    lengths,
    attn_gain,
    w_query,
    w_key,
    w_value,
    w_out,
    final_gain,
    lm_head,
):
    groups = lax.axis_size("fsdp")
    seq_count = lax.axis_size("seq")
    group_index = lax.axis_index("fsdp")
    seq_index = lax.axis_index("seq")
    seq_len = text_embeds.shape[0]
    width = text_embeds.shape[1]
    columns = w_key.shape[1]
    heads_local = columns // HD
    dpiece = width // groups
    fpiece = width // seq_count
    quarter = groups // seq_count
    capacity = max(2, 2 * vision_tokens.shape[0] // groups)
    last_index = lengths[0] - 1
    destination = vision_request[:, 0]
    onehot = (destination[:, None] == jnp.arange(groups, dtype=jnp.int32)[None, :]).astype(
        jnp.int32
    )
    slot_index = jnp.sum((jnp.cumsum(onehot, axis=0) - onehot) * onehot, axis=1)
    counts = jnp.sum(onehot, axis=0)
    outbox = pack_slots(vision_tokens, destination, slot_index, groups, capacity)
    final_text = lax.dynamic_slice_in_dim(text_embeds, last_index, 1, 0)
    last_row = row_norm(final_text, attn_gain)
    last_pieces = jnp.stack(
        [last_row.reshape(groups, dpiece), final_text.reshape(groups, dpiece)], axis=1
    )
    last_parts = lax.all_to_all(last_pieces, "fsdp", split_axis=0, concat_axis=0, tiled=True)
    received = lax.all_to_all(outbox, "fsdp", split_axis=0, concat_axis=0, tiled=True)
    arrived = lax.all_to_all(counts[:, None], "fsdp", split_axis=0, concat_axis=0, tiled=True)
    query = lax.psum(
        jnp.dot(last_parts[:, 0], w_query, preferred_element_type=jnp.float32), "fsdp"
    ).astype(jnp.bfloat16)
    gain_part = lax.dynamic_slice_in_dim(attn_gain, group_index * dpiece, dpiece, 0)
    probe_part = (
        jnp.einsum(
            "rhc,dhc->rhd",
            query.reshape(groups, heads_local, HD),
            w_key.reshape(dpiece, heads_local, HD),
            preferred_element_type=jnp.float32,
        )
        * gain_part
    ).astype(jnp.bfloat16)
    probe = lax.all_to_all(probe_part, "fsdp", split_axis=0, concat_axis=0, tiled=True)
    probe = probe.transpose(1, 0, 2).reshape(heads_local, width)
    probe = lax.all_to_all(probe, "seq", split_axis=1, concat_axis=0, tiled=True)
    occupied = (
        (jnp.arange(capacity, dtype=jnp.int32)[None, :] < arrived).astype(jnp.int32).reshape(-1)
    )
    ranking = jnp.cumsum(occupied) - occupied
    positions = jnp.where(occupied > 0, image_start[0] + ranking, seq_len)
    text_piece = lax.dynamic_slice_in_dim(text_embeds, seq_index * fpiece, fpiece, 1)
    states = text_piece.at[positions].set(received.reshape(-1, fpiece), mode="drop")
    widened = states.astype(jnp.float32)
    squares = jnp.sum(widened * widened, axis=1)
    partial_scores = jnp.einsum("hd,jd->hj", probe, states, preferred_element_type=jnp.float32)
    summed = lax.psum(jnp.concatenate([partial_scores, squares[None, :]], axis=0), "seq")
    inverse = lax.rsqrt(summed[-1:] / width + norm_epsilon)
    scores = summed[:-1] * inverse / math.sqrt(HD)
    live_keys = jnp.arange(seq_len, dtype=jnp.int32) < lengths[0]
    scores = jnp.where(live_keys[None, :], scores, -jnp.inf)
    peak = jnp.max(scores, axis=1, keepdims=True)
    shifted = jnp.exp(scores - peak)
    weights = shifted / jnp.sum(shifted, axis=1, keepdims=True)
    mixed = jnp.dot(
        (weights * inverse).astype(jnp.bfloat16), states, preferred_element_type=jnp.float32
    )
    mixed_gain = lax.dynamic_slice_in_dim(attn_gain, seq_index * fpiece, fpiece, 0)
    mixed = (mixed * mixed_gain).astype(jnp.bfloat16)
    mixed = lax.all_to_all(mixed, "seq", split_axis=0, concat_axis=1, tiled=True)
    mixed = mixed.reshape(heads_local, groups, dpiece).transpose(1, 0, 2)
    mixed = lax.all_to_all(mixed, "fsdp", split_axis=0, concat_axis=0, tiled=True)
    attended = lax.psum(
        jnp.einsum(
            "rhd,dhc->rhc",
            mixed,
            w_value.reshape(dpiece, heads_local, HD),
            preferred_element_type=jnp.float32,
        ).reshape(groups, columns),
        "fsdp",
    ).astype(jnp.bfloat16)
    out_rows = lax.dynamic_slice_in_dim(w_out, seq_index * columns, columns, 0)
    projected = lax.psum(jnp.dot(attended, out_rows, preferred_element_type=jnp.float32), "seq")
    residual_out = last_parts[:, 1].astype(jnp.float32) + projected
    residual_out = lax.dynamic_slice_in_dim(residual_out, seq_index * quarter, quarter, 0)
    final_part = lax.dynamic_slice_in_dim(final_gain, group_index * dpiece, dpiece, 0)
    scaled_out = (residual_out * final_part[None, :]).astype(jnp.bfloat16)
    square_part = jnp.sum(residual_out * residual_out, axis=1)
    full_scaled = lax.all_gather(scaled_out, "fsdp", axis=1, tiled=True)
    mean_square = lax.psum(square_part, "fsdp") / width
    logits = jnp.dot(full_scaled, lm_head, preferred_element_type=jnp.float32)
    local_max = jnp.max(logits, axis=1) * lax.rsqrt(mean_square + norm_epsilon)
    max_logit = lax.pmax(local_max, "fsdp")
    return (jnp.sqrt(mean_square), max_logit)


MESH = pl.DeviceIdType.MESH
F32 = jnp.float32
BF16 = jnp.bfloat16


def dot(a, b):
    return jnp.dot(a, b, preferred_element_type=F32)


def dot_rows(a, b):
    return lax.dot_general(a, b, (((1,), (1,)), ((), ())), preferred_element_type=F32)


def iota(shape, axis):
    return lax.broadcasted_iota(jnp.int32, shape, axis)


def folded(rows):
    half = rows.shape[1] // 2
    return jnp.concatenate([rows[:, :half], rows[:, half:]], axis=0).astype(BF16)


def unfolded(rows):
    half = rows.shape[0] // 2
    return jnp.concatenate([rows[:half], rows[half:]], axis=1)


def wrap(index, size):
    return jnp.where(index >= size, index - size, index)


def fused_kernel(
    groups,
    seq_count,
    capacity,
    request,
    start,
    lengths,
    attn_gain,
    final_gain,
    text_hbm,
    vision_hbm,
    wq_hbm,
    wk_hbm,
    wv_hbm,
    wo_hbm,
    lm_hbm,
    rms_out,
    max_out,
    text,
    vision,
    wq,
    wk,
    wv,
    wo,
    lm,
    states,
    heads_in,
    stage,
    last_send,
    last_recv,
    box_send,
    box_recv,
    query_send,
    query_recv,
    key_send,
    key_recv,
    score_recv,
    mix_send,
    mix_recv,
    att_send,
    att_recv,
    out_recv,
    scaled_send,
    scaled_recv,
    peak_send,
    peak_recv,
    local_sem,
    send_sem,
    recv_sem,
):
    f = lax.axis_index("fsdp")
    s = lax.axis_index("seq")
    devices = groups * seq_count
    seq_len, width = text.shape
    rows_per = width // groups
    piece = width // seq_count
    owners = groups // seq_count
    columns = wq.shape[1]
    local_heads = columns // HD
    heads = local_heads * seq_count
    vtok = vision.shape[0]
    half = rows_per // 2
    chunks = rows_per // 128

    barrier = pltpu.get_barrier_semaphore()
    me = f * seq_count + s

    others = []
    for k in range(groups):
        for j in range(seq_count):
            if k or j:
                others.append((wrap(f + k, groups), wrap(s + j, seq_count)))
    for other in others:
        pl.semaphore_signal(barrier, inc=1, device_id=other, device_id_type=MESH)

    def fetch(index, source, target):
        copy = pltpu.make_async_copy(source, target, local_sem.at[index])
        copy.start()
        return copy

    get_text = fetch(0, text_hbm, text)
    get_vision = fetch(1, vision_hbm, vision)
    get_wq = fetch(2, wq_hbm, wq)
    get_wk = fetch(3, wk_hbm, wk)

    sent = []

    def copy_of(phase, slot, from_slot, source, target, to_f, to_s):
        return pltpu.make_async_remote_copy(
            src_ref=source,
            dst_ref=target,
            send_sem=send_sem.at[phase, slot],
            recv_sem=recv_sem.at[phase, from_slot],
            device_id=(to_f, to_s),
            device_id_type=MESH,
        )

    def push(*what):
        copy = copy_of(*what)
        copy.start()
        sent.append(copy)

    def arrive(phase, slot, target):
        copy_of(phase, 0, slot, target, target, f, s).wait_recv()

    def across_groups(phase, source, target):
        for k in range(1, groups):
            t = wrap(f + k, groups)
            push(phase, k, f, source(t), target(f), t, s)

    def from_groups(phase, target):
        for k in range(1, groups):
            o = wrap(f + groups - k, groups)
            arrive(phase, o, target(o))

    def across_seq(phase, source, target):
        for k in range(1, seq_count):
            t = wrap(s + k, seq_count)
            push(phase, k, s, source(t), target(s), f, t)

    def from_seq(phase, target):
        for k in range(1, seq_count):
            o = wrap(s + seq_count - k, seq_count)
            arrive(phase, o, target(o))

    length = lengths[0]
    tail = (seq_len - 8) // 16 * 16
    get_text.wait()
    get_wv = fetch(4, wv_hbm, wv)
    get_wo = fetch(5, wo_hbm.at[pl.ds(pl.multiple_of(s * columns, columns), columns)], wo)
    words = lm.shape[0]
    vocab = lm_hbm.shape[0]
    final_seq = s == seq_count - 1
    final_words = vocab - (seq_count - 1) * words
    get_lm = pltpu.make_async_copy(
        lm_hbm.at[pl.ds(pl.multiple_of(s * words, words), words)], lm, local_sem.at[6]
    )
    get_lm_final = pltpu.make_async_copy(
        lm_hbm.at[vocab - final_words :], lm.at[:final_words], local_sem.at[6]
    )

    @pl.when(jnp.logical_not(final_seq))
    def _():
        get_lm.start()

    @pl.when(final_seq)
    def _():
        get_lm_final.start()
        if final_words < words:
            lm[final_words:, :] = jnp.zeros((words - final_words, width), BF16)

    tail_rows = text[tail:, :].astype(F32)
    here = iota((seq_len - tail, 1), 0) == length - 1 - tail
    last = jnp.sum(jnp.where(here, tail_rows, 0.0), axis=0, keepdims=True)
    scale = lax.rsqrt(jnp.mean(last * last, axis=1, keepdims=True) + norm_epsilon)
    normed = (last * scale * attn_gain[...]).astype(BF16).astype(F32)
    named = request[...]
    member = jnp.where(iota((groups, vtok), 0) == named, 1.0, 0.0)
    counts = jnp.broadcast_to(jnp.sum(member, axis=1, keepdims=True), (groups, rows_per))
    for g in range(groups):
        span = slice(g * rows_per, (g + 1) * rows_per)
        last_send[g, 0:1, :] = normed[:, span]
        last_send[g, 1:2, :] = last[:, span]
        last_send[g, 2:3, :] = counts[g : g + 1, :]
    last_recv[f] = last_send[f]

    earlier = jnp.where(iota((vtok, vtok), 0) < iota((vtok, vtok), 1), 1.0, 0.0)
    before = dot(member.astype(BF16), earlier.astype(BF16))
    rank = jnp.sum(before * member, axis=0, keepdims=True)
    slot = named.astype(F32) * capacity + rank
    slots = groups * capacity
    pick = jnp.where(iota((slots, vtok), 0).astype(F32) == slot, 1.0, 0.0).astype(BF16)
    get_vision.wait()
    box_send[...] = dot(pick, vision[...]).astype(BF16).reshape(groups, capacity, piece)
    box_recv[f] = box_send[f]
    pl.semaphore_wait(barrier, devices - 1)
    across_groups(0, lambda t: last_send.at[t], lambda me_f: last_recv.at[me_f])

    across_groups(2, lambda t: box_send.at[t], lambda me_f: box_recv.at[me_f])

    from_groups(0, lambda o: last_recv.at[o])
    get_wq.wait()
    query_part = dot(last_recv[:, 0, :].astype(BF16), wq[...])
    query_send[...] = folded(query_part)
    query_recv[f] = query_send[...]
    across_groups(3, lambda t: query_send, lambda me_f: query_recv.at[me_f])
    get_wk.wait()
    from_groups(3, lambda o: query_recv.at[o])
    query = unfolded(jnp.sum(query_recv[...].astype(F32), axis=0)).astype(BF16)

    gain_rows = attn_gain[:, pl.ds(pl.multiple_of(f * rows_per, rows_per), rows_per)]
    for h in range(local_heads):
        span = slice(h * HD, (h + 1) * HD)
        probe = dot_rows(query[:, span], wk[:, span]) * gain_rows
        for c in range(chunks):
            stage[:, c * local_heads + h, :] = probe[:, c * 128 : (c + 1) * 128]
    key_send[...] = stage[...].astype(BF16)
    home = lax.div(f, owners)
    inner = lax.rem(f, owners)
    at_home = home == s
    own_key = copy_of(4, 0, inner * seq_count + s, key_send.at[f], key_recv.at[inner, s], f, home)

    @pl.when(at_home)
    def _():
        key_recv[inner, s] = key_send[f]

    @pl.when(jnp.logical_not(at_home))
    def _():
        own_key.start()

    for k in range(1, groups):
        t = wrap(f + k, groups)
        push(4, k, inner * seq_count + s, key_send.at[t], key_recv.at[inner, s], t, home)

    tally = last_recv[:, 2, :128]
    tallies = jnp.concatenate([tally] * (slots // 128), axis=1)
    source_of = iota((groups, slots), 0)
    owner = lax.div(iota((groups, slots), 1), capacity)
    arrived = jnp.sum(jnp.where(source_of == owner, tallies, 0.0), axis=0, keepdims=True)
    offset = jnp.sum(jnp.where(source_of < owner, tallies, 0.0), axis=0, keepdims=True)
    within = lax.rem(iota((1, slots), 1), capacity).astype(F32)
    first = start[0].astype(F32)
    position = jnp.where(within < arrived, first + offset + within, -1.0)
    place = jnp.where(iota((seq_len, slots), 0).astype(F32) == position, 1.0, 0.0).astype(BF16)
    total = jnp.sum(tally[:, :1], axis=0, keepdims=True)
    row = iota((seq_len, 1), 0).astype(F32)
    taken = jnp.logical_and(row >= first, row < first + total)
    from_groups(2, lambda o: box_recv.at[o])
    step = min(256, piece)
    squares = jnp.zeros((seq_len, 1), F32)
    for c in range(piece // step):
        span = slice(c * step, (c + 1) * step)
        placed = dot(place, box_recv[:, :, span].reshape(slots, step))
        at = pl.multiple_of(s * piece + c * step, step)
        value = jnp.where(taken, placed, text[:, pl.ds(at, step)].astype(F32))
        states[:, span] = value.astype(BF16)
        squares = squares + jnp.sum(value * value, axis=1, keepdims=True)

    for b in range(owners):
        for k in range(seq_count):
            o = wrap(s + k, seq_count)
            if k:
                arrive(4, b * seq_count + o, key_recv.at[b, o])
            else:

                @pl.when(jnp.logical_not(f == s * owners + b))
                def _(o=o, b=b):
                    arrive(4, b * seq_count + o, key_recv.at[b, o])

    for o in range(seq_count):
        for b in range(owners):
            block = key_recv[b, o].astype(F32)
            for c in range(chunks):
                at = b * rows_per + c * 128
                heads_in[o * local_heads : (o + 1) * local_heads, at : at + 128] = block[
                    c * local_heads : (c + 1) * local_heads
                ]
    heads_in[heads:, :] = jnp.zeros((8, piece), F32)
    part = dot_rows(states[...], heads_in[...].astype(BF16))
    part = jnp.where(iota((1, heads + 8), 1) == heads, squares, part)
    score_recv[s] = part.T
    across_seq(5, lambda t: score_recv.at[s], lambda me_s: score_recv.at[me_s])
    from_seq(5, lambda o: score_recv.at[o])
    summed = jnp.sum(score_recv[...], axis=0)
    inverse = lax.rsqrt(summed[heads : heads + 1] / width + norm_epsilon)
    live = iota((1, seq_len), 1) < length
    scores = jnp.where(live, summed[:heads] * inverse / math.sqrt(HD), -jnp.inf)
    shifted = jnp.exp(scores - jnp.max(scores, axis=1, keepdims=True))
    weights = shifted / jnp.sum(shifted, axis=1, keepdims=True)
    mixed = dot((weights * inverse).astype(BF16), states[...])
    mixed = mixed * attn_gain[:, pl.ds(pl.multiple_of(s * piece, piece), piece)]

    for o in range(seq_count):
        for b in range(owners):
            rows = mixed[o * local_heads : (o + 1) * local_heads]
            starts = [b * rows_per + c * 128 for c in range(chunks)]
            mix_send[b, o] = jnp.concatenate(
                [rows[:, at : at + 128] for at in starts], axis=0
            ).astype(BF16)
    own_mix = []
    for b in range(owners):
        t = s * owners + b
        copy = copy_of(6, b * seq_count, f, mix_send.at[b, s], mix_recv.at[f], t, s)
        own_mix.append((t, copy))

        @pl.when(f == t)
        def _(b=b):
            mix_recv[f] = mix_send[b, s]

        @pl.when(jnp.logical_not(f == t))
        def _(copy=copy):
            copy.start()

        for k in range(1, seq_count):
            o = wrap(s + k, seq_count)
            push(6, b * seq_count + k, f, mix_send.at[b, o], mix_recv.at[f], t, o)
    get_wv.wait()
    from_groups(6, lambda o: mix_recv.at[o])

    @pl.when(jnp.logical_not(at_home))
    def _():
        arrive(6, f, mix_recv.at[f])

    stage[...] = mix_recv[...].astype(F32)
    att_part = []
    for h in range(local_heads):
        rows = [stage[:, c * local_heads + h, :] for c in range(chunks)]
        rows = jnp.concatenate(rows, axis=1).astype(BF16)
        att_part.append(dot(rows, wv[:, h * HD : (h + 1) * HD]))
    att_send[...] = folded(jnp.concatenate(att_part, axis=1))
    att_recv[f] = att_send[...]
    across_groups(7, lambda t: att_send, lambda me_f: att_recv.at[me_f])
    get_wo.wait()
    from_groups(7, lambda o: att_recv.at[o])
    attended = unfolded(jnp.sum(att_recv[...].astype(F32), axis=0)).astype(BF16)

    out_recv[s] = dot(attended, wo[...])
    across_seq(8, lambda t: out_recv.at[s], lambda me_s: out_recv.at[me_s])
    from_seq(8, lambda o: out_recv.at[o])
    residual = last_recv[:, 1, :] + jnp.sum(out_recv[...], axis=0)
    square_part = jnp.sum(residual * residual, axis=1, keepdims=True)
    final_rows = final_gain[:, pl.ds(pl.multiple_of(f * rows_per, rows_per), rows_per)]
    scaled = residual * final_rows
    scaled_send[...] = folded(scaled)

    scaled_recv[f] = scaled_send[...]
    across_groups(9, lambda t: scaled_send, lambda me_f: scaled_recv.at[me_f])

    @pl.when(jnp.logical_not(final_seq))
    def _():
        get_lm.wait()

    @pl.when(final_seq)
    def _():
        get_lm_final.wait()

    from_groups(9, lambda o: scaled_recv.at[o])
    scaled_full = jnp.concatenate([unfolded(scaled_recv[o]) for o in range(groups)], axis=1)
    logits = dot_rows(lm[...], scaled_full)
    word = iota((words, 1), 0) + s * words
    top = jnp.max(jnp.where(word < vocab, logits, -jnp.inf), axis=0, keepdims=True)
    diagonal = iota((groups, groups), 0) == iota((groups, groups), 1)
    top = jnp.max(jnp.where(diagonal, top, -jnp.inf), axis=1, keepdims=True)
    peaks = jnp.where(iota((groups, 128), 1) < 64, top, square_part)
    for o in range(seq_count):
        peak_send[o] = peaks[o * owners : (o + 1) * owners]
    peak_recv[me] = peak_send[s]
    for k, (t_f, t_s) in enumerate(others):
        push(10, k, me, peak_send.at[t_s], peak_recv.at[me], t_f, t_s)
    for t_f, t_s in others:
        o = t_f * seq_count + t_s
        arrive(10, o, peak_recv.at[o])
    everyone = peak_recv[...]
    best = jnp.max(everyone, axis=0)[:, :1]
    mean_square = jnp.sum(everyone, axis=0)[:, 64:65] / (width * seq_count)
    rms_out[...] = jnp.broadcast_to(jnp.sqrt(mean_square), (owners, 128))
    max_out[...] = jnp.broadcast_to(best * lax.rsqrt(mean_square + norm_epsilon), (owners, 128))

    for copy in sent:
        copy.wait_send()

    @pl.when(jnp.logical_not(at_home))
    def _():
        own_key.wait_send()

    for t, copy in own_mix:

        @pl.when(jnp.logical_not(f == t))
        def _(copy=copy):
            copy.wait_send()


def fused(
    text_embeds,
    vision_tokens,
    vision_request,
    image_start,
    lengths,
    attn_gain,
    w_query,
    w_key,
    w_value,
    w_out,
    final_gain,
    lm_head,
):
    groups = lax.axis_size("fsdp")
    seq_count = lax.axis_size("seq")
    seq_len, width = text_embeds.shape
    vtok, piece = vision_tokens.shape
    rows_per, columns = w_query.shape
    words = -(-lm_head.shape[1] // (16 * seq_count)) * 16
    owners = groups // seq_count
    local_heads = columns // HD
    heads = local_heads * seq_count
    capacity = 2 * vtok // groups
    vmem = pl.BlockSpec(memory_space=pltpu.VMEM)
    smem = pl.BlockSpec(memory_space=pltpu.SMEM)
    any_space = pl.BlockSpec(memory_space=pl.ANY)
    phases = 12
    links = groups * seq_count
    rms, best = pl.pallas_call(
        functools.partial(fused_kernel, groups, seq_count, capacity),
        out_shape=[jax.ShapeDtypeStruct((owners, 128), F32)] * 2,
        in_specs=[vmem, smem, smem, vmem, vmem] + [any_space] * 7,
        out_specs=[vmem, vmem],
        scratch_shapes=[
            pltpu.VMEM((seq_len, width), BF16),
            pltpu.VMEM((vtok, piece), BF16),
            pltpu.VMEM((rows_per, columns), BF16),
            pltpu.VMEM((rows_per, columns), BF16),
            pltpu.VMEM((rows_per, columns), BF16),
            pltpu.VMEM((columns, rows_per), BF16),
            pltpu.VMEM((words, width), BF16),
            pltpu.VMEM((seq_len, piece), BF16),
            pltpu.VMEM((heads + 8, piece), F32),
            pltpu.VMEM((groups, local_heads * rows_per // 128, 128), F32),
            pltpu.VMEM((groups, 3, rows_per), F32),
            pltpu.VMEM((groups, 3, rows_per), F32),
            pltpu.VMEM((groups, capacity, piece), BF16),
            pltpu.VMEM((groups, capacity, piece), BF16),
            pltpu.VMEM((2 * groups, columns // 2), BF16),
            pltpu.VMEM((groups, 2 * groups, columns // 2), BF16),
            pltpu.VMEM((groups, local_heads * rows_per // 128, 128), BF16),
            pltpu.VMEM((owners, seq_count, local_heads * rows_per // 128, 128), BF16),
            pltpu.VMEM((seq_count, heads + 8, seq_len), F32),
            pltpu.VMEM((owners, seq_count, local_heads * rows_per // 128, 128), BF16),
            pltpu.VMEM((groups, local_heads * rows_per // 128, 128), BF16),
            pltpu.VMEM((2 * groups, columns // 2), BF16),
            pltpu.VMEM((groups, 2 * groups, columns // 2), BF16),
            pltpu.VMEM((seq_count, groups, rows_per), F32),
            pltpu.VMEM((2 * groups, rows_per // 2), BF16),
            pltpu.VMEM((groups, 2 * groups, rows_per // 2), BF16),
            pltpu.VMEM((seq_count, owners, 128), F32),
            pltpu.VMEM((groups * seq_count, owners, 128), F32),
            pltpu.SemaphoreType.DMA((7,)),
            pltpu.SemaphoreType.DMA((phases, links)),
            pltpu.SemaphoreType.DMA((phases, links)),
        ],
        compiler_params=pltpu.CompilerParams(
            collective_id=0, has_side_effects=True, vmem_limit_bytes=56 * 2**20
        ),
        name="fused",
    )(
        vision_request.reshape(1, vtok),
        image_start,
        lengths,
        attn_gain.reshape(1, width),
        final_gain.reshape(1, width),
        text_embeds,
        vision_tokens,
        w_query,
        w_key,
        w_value,
        w_out,
        lm_head.T,
    )
    return rms[:, 0], best[:, 0]


def fits(mesh):
    groups, seq_count = mesh.shape["fsdp"], mesh.shape["seq"]
    return groups == 8 and groups % seq_count == 0


def solution(mesh):
    return jax.shard_map(
        fused if fits(mesh) else local,
        mesh=mesh,
        in_specs=(
            P("fsdp", None),
            P("fsdp", "seq"),
            P("fsdp", None),
            P("fsdp"),
            P("fsdp"),
            P(),
            P("fsdp", "seq"),
            P("fsdp", "seq"),
            P("fsdp", "seq"),
            P(None, "fsdp"),
            P(),
            P(None, "fsdp"),
        ),
        out_specs=(P("seq"), P("seq")),
        check_vma=False,
    )
```

```python
import functools
import math

import jax
import jax.numpy as jnp
from jax import lax
from jax.experimental import pallas as pl
from jax.experimental.pallas import tpu as pltpu
from jax.sharding import PartitionSpec as P

HD = 128


norm_epsilon = 1e-05


def row_norm(rows, gain):
    widened = rows.astype(jnp.float32)
    return (
        widened
        * lax.rsqrt(jnp.mean(widened * widened, axis=1, keepdims=True) + norm_epsilon)
        * gain
    ).astype(jnp.bfloat16)


def pack_slots(tokens, destination, slot_index, groups, capacity):
    return (
        jnp.zeros((groups, capacity, tokens.shape[1]), jnp.bfloat16)
        .at[destination, slot_index]
        .set(tokens)
    )


def local(
    text_embeds,
    vision_tokens,
    vision_request,
    image_start,
    lengths,
    attn_gain,
    w_query,
    w_key,
    w_value,
    w_out,
    final_gain,
    lm_head,
):
    groups = lax.axis_size("fsdp")
    seq_count = lax.axis_size("seq")
    group_index = lax.axis_index("fsdp")
    seq_index = lax.axis_index("seq")
    seq_len = text_embeds.shape[0]
    width = text_embeds.shape[1]
    columns = w_key.shape[1]
    heads_local = columns // HD
    dpiece = width // groups
    fpiece = width // seq_count
    quarter = groups // seq_count
    capacity = max(2, 2 * vision_tokens.shape[0] // groups)
    last_index = lengths[0] - 1
    destination = vision_request[:, 0]
    onehot = (destination[:, None] == jnp.arange(groups, dtype=jnp.int32)[None, :]).astype(
        jnp.int32
    )
    slot_index = jnp.sum((jnp.cumsum(onehot, axis=0) - onehot) * onehot, axis=1)
    counts = jnp.sum(onehot, axis=0)
    outbox = pack_slots(vision_tokens, destination, slot_index, groups, capacity)
    final_text = lax.dynamic_slice_in_dim(text_embeds, last_index, 1, 0)
    last_row = row_norm(final_text, attn_gain)
    last_pieces = jnp.stack(
        [last_row.reshape(groups, dpiece), final_text.reshape(groups, dpiece)], axis=1
    )
    last_parts = lax.all_to_all(last_pieces, "fsdp", split_axis=0, concat_axis=0, tiled=True)
    received = lax.all_to_all(outbox, "fsdp", split_axis=0, concat_axis=0, tiled=True)
    arrived = lax.all_to_all(counts[:, None], "fsdp", split_axis=0, concat_axis=0, tiled=True)
    query = lax.psum(
        jnp.dot(last_parts[:, 0], w_query, preferred_element_type=jnp.float32), "fsdp"
    ).astype(jnp.bfloat16)
    gain_part = lax.dynamic_slice_in_dim(attn_gain, group_index * dpiece, dpiece, 0)
    probe_part = (
        jnp.einsum(
            "rhc,dhc->rhd",
            query.reshape(groups, heads_local, HD),
            w_key.reshape(dpiece, heads_local, HD),
            preferred_element_type=jnp.float32,
        )
        * gain_part
    ).astype(jnp.bfloat16)
    probe = lax.all_to_all(probe_part, "fsdp", split_axis=0, concat_axis=0, tiled=True)
    probe = probe.transpose(1, 0, 2).reshape(heads_local, width)
    probe = lax.all_to_all(probe, "seq", split_axis=1, concat_axis=0, tiled=True)
    occupied = (
        (jnp.arange(capacity, dtype=jnp.int32)[None, :] < arrived).astype(jnp.int32).reshape(-1)
    )
    ranking = jnp.cumsum(occupied) - occupied
    positions = jnp.where(occupied > 0, image_start[0] + ranking, seq_len)
    text_piece = lax.dynamic_slice_in_dim(text_embeds, seq_index * fpiece, fpiece, 1)
    states = text_piece.at[positions].set(received.reshape(-1, fpiece), mode="drop")
    widened = states.astype(jnp.float32)
    squares = jnp.sum(widened * widened, axis=1)
    partial_scores = jnp.einsum("hd,jd->hj", probe, states, preferred_element_type=jnp.float32)
    summed = lax.psum(jnp.concatenate([partial_scores, squares[None, :]], axis=0), "seq")
    inverse = lax.rsqrt(summed[-1:] / width + norm_epsilon)
    scores = summed[:-1] * inverse / math.sqrt(HD)
    live_keys = jnp.arange(seq_len, dtype=jnp.int32) < lengths[0]
    scores = jnp.where(live_keys[None, :], scores, -jnp.inf)
    peak = jnp.max(scores, axis=1, keepdims=True)
    shifted = jnp.exp(scores - peak)
    weights = shifted / jnp.sum(shifted, axis=1, keepdims=True)
    mixed = jnp.dot(
        (weights * inverse).astype(jnp.bfloat16), states, preferred_element_type=jnp.float32
    )
    mixed_gain = lax.dynamic_slice_in_dim(attn_gain, seq_index * fpiece, fpiece, 0)
    mixed = (mixed * mixed_gain).astype(jnp.bfloat16)
    mixed = lax.all_to_all(mixed, "seq", split_axis=0, concat_axis=1, tiled=True)
    mixed = mixed.reshape(heads_local, groups, dpiece).transpose(1, 0, 2)
    mixed = lax.all_to_all(mixed, "fsdp", split_axis=0, concat_axis=0, tiled=True)
    attended = lax.psum(
        jnp.einsum(
            "rhd,dhc->rhc",
            mixed,
            w_value.reshape(dpiece, heads_local, HD),
            preferred_element_type=jnp.float32,
        ).reshape(groups, columns),
        "fsdp",
    ).astype(jnp.bfloat16)
    out_rows = lax.dynamic_slice_in_dim(w_out, seq_index * columns, columns, 0)
    projected = lax.psum(jnp.dot(attended, out_rows, preferred_element_type=jnp.float32), "seq")
    residual_out = last_parts[:, 1].astype(jnp.float32) + projected
    residual_out = lax.dynamic_slice_in_dim(residual_out, seq_index * quarter, quarter, 0)
    final_part = lax.dynamic_slice_in_dim(final_gain, group_index * dpiece, dpiece, 0)
    scaled_out = (residual_out * final_part[None, :]).astype(jnp.bfloat16)
    square_part = jnp.sum(residual_out * residual_out, axis=1)
    full_scaled = lax.all_gather(scaled_out, "fsdp", axis=1, tiled=True)
    mean_square = lax.psum(square_part, "fsdp") / width
    logits = jnp.dot(full_scaled, lm_head, preferred_element_type=jnp.float32)
    local_max = jnp.max(logits, axis=1) * lax.rsqrt(mean_square + norm_epsilon)
    max_logit = lax.pmax(local_max, "fsdp")
    return (jnp.sqrt(mean_square), max_logit)


MESH = pl.DeviceIdType.MESH
F32 = jnp.float32
BF16 = jnp.bfloat16


def dot(a, b):
    return jnp.dot(a, b, preferred_element_type=F32)


def dot_rows(a, b):
    return lax.dot_general(a, b, (((1,), (1,)), ((), ())), preferred_element_type=F32)


def iota(shape, axis):
    return lax.broadcasted_iota(jnp.int32, shape, axis)


def folded(rows):
    half = rows.shape[1] // 2
    return jnp.concatenate([rows[:, :half], rows[:, half:]], axis=0).astype(BF16)


def unfolded(rows):
    half = rows.shape[0] // 2
    return jnp.concatenate([rows[:half], rows[half:]], axis=1)


def wrap(index, size):
    return jnp.where(index >= size, index - size, index)


def fused_kernel(
    groups,
    seq_count,
    capacity,
    request,
    start,
    lengths,
    attn_gain,
    final_gain,
    text_hbm,
    vision_hbm,
    wq_hbm,
    wk_hbm,
    wv_hbm,
    wo_hbm,
    lm_hbm,
    rms_out,
    max_out,
    text,
    vision,
    wq,
    wk,
    wv,
    wo,
    lm,
    states,
    heads_in,
    stage,
    last_send,
    last_recv,
    box_send,
    box_recv,
    query_send,
    query_recv,
    key_send,
    key_recv,
    score_recv,
    mix_send,
    mix_recv,
    att_send,
    att_recv,
    out_recv,
    scaled_send,
    scaled_recv,
    peak_send,
    peak_row,
    peak_recv,
    local_sem,
    send_sem,
    recv_sem,
):
    f = lax.axis_index("fsdp")
    s = lax.axis_index("seq")
    devices = groups * seq_count
    seq_len, width = text.shape
    rows_per = width // groups
    piece = width // seq_count
    owners = groups // seq_count
    columns = wq.shape[1]
    local_heads = columns // HD
    heads = local_heads * seq_count
    vtok = vision.shape[0]
    half = rows_per // 2
    chunks = rows_per // 128

    barrier = pltpu.get_barrier_semaphore()
    me = f * seq_count + s

    others = []
    for k in range(groups):
        for j in range(seq_count):
            if k or j:
                others.append((wrap(f + k, groups), wrap(s + j, seq_count)))
    for other in others:
        pl.semaphore_signal(barrier, inc=1, device_id=other, device_id_type=MESH)

    def fetch(index, source, target):
        copy = pltpu.make_async_copy(source, target, local_sem.at[index])
        copy.start()
        return copy

    get_text = fetch(0, text_hbm, text)
    get_vision = fetch(1, vision_hbm, vision)
    get_wq = fetch(2, wq_hbm, wq)
    get_wk = fetch(3, wk_hbm, wk)

    sent = []

    def copy_of(phase, slot, from_slot, source, target, to_f, to_s):
        return pltpu.make_async_remote_copy(
            src_ref=source,
            dst_ref=target,
            send_sem=send_sem.at[phase, slot],
            recv_sem=recv_sem.at[phase, from_slot],
            device_id=(to_f, to_s),
            device_id_type=MESH,
        )

    def push(*what):
        copy = copy_of(*what)
        copy.start()
        sent.append(copy)

    def arrive(phase, slot, target):
        copy_of(phase, 0, slot, target, target, f, s).wait_recv()

    def across_groups(phase, source, target):
        for k in range(1, groups):
            t = wrap(f + k, groups)
            push(phase, k, f, source(t), target(f), t, s)

    def from_groups(phase, target):
        for k in range(1, groups):
            o = wrap(f + groups - k, groups)
            arrive(phase, o, target(o))

    def across_seq(phase, source, target):
        for k in range(1, seq_count):
            t = wrap(s + k, seq_count)
            push(phase, k, s, source(t), target(s), f, t)

    def from_seq(phase, target):
        for k in range(1, seq_count):
            o = wrap(s + seq_count - k, seq_count)
            arrive(phase, o, target(o))

    length = lengths[0]
    tail = (seq_len - 8) // 16 * 16
    get_text.wait()
    get_wv = fetch(4, wv_hbm, wv)
    get_wo = fetch(5, wo_hbm.at[pl.ds(pl.multiple_of(s * columns, columns), columns)], wo)
    words = lm.shape[0]
    vocab = lm_hbm.shape[0]
    final_seq = s == seq_count - 1
    final_words = vocab - (seq_count - 1) * words
    get_lm = pltpu.make_async_copy(
        lm_hbm.at[pl.ds(pl.multiple_of(s * words, words), words)], lm, local_sem.at[6]
    )
    get_lm_final = pltpu.make_async_copy(
        lm_hbm.at[vocab - final_words :], lm.at[:final_words], local_sem.at[6]
    )

    @pl.when(jnp.logical_not(final_seq))
    def _():
        get_lm.start()

    @pl.when(final_seq)
    def _():
        get_lm_final.start()
        if final_words < words:
            lm[final_words:, :] = jnp.zeros((words - final_words, width), BF16)

    tail_rows = text[tail:, :].astype(F32)
    here = iota((seq_len - tail, 1), 0) == length - 1 - tail
    last = jnp.sum(jnp.where(here, tail_rows, 0.0), axis=0, keepdims=True)
    scale = lax.rsqrt(jnp.mean(last * last, axis=1, keepdims=True) + norm_epsilon)
    normed = (last * scale * attn_gain[...]).astype(BF16).astype(F32)
    named = request[...]
    member = jnp.where(iota((groups, vtok), 0) == named, 1.0, 0.0)
    counts = jnp.broadcast_to(jnp.sum(member, axis=1, keepdims=True), (groups, rows_per))
    for g in range(groups):
        span = slice(g * rows_per, (g + 1) * rows_per)
        last_send[g, 0:1, :] = normed[:, span]
        last_send[g, 1:2, :] = last[:, span]
        last_send[g, 2:3, :] = counts[g : g + 1, :]
    last_recv[f] = last_send[f]

    earlier = jnp.where(iota((vtok, vtok), 0) < iota((vtok, vtok), 1), 1.0, 0.0)
    before = dot(member.astype(BF16), earlier.astype(BF16))
    rank = jnp.sum(before * member, axis=0, keepdims=True)
    slot = named.astype(F32) * capacity + rank
    slots = groups * capacity
    pick = jnp.where(iota((slots, vtok), 0).astype(F32) == slot, 1.0, 0.0).astype(BF16)
    get_vision.wait()
    box_send[...] = dot(pick, vision[...]).astype(BF16).reshape(groups, capacity, piece)
    box_recv[f] = box_send[f]
    pl.semaphore_wait(barrier, devices - 1)
    across_groups(0, lambda t: last_send.at[t], lambda me_f: last_recv.at[me_f])

    across_groups(2, lambda t: box_send.at[t], lambda me_f: box_recv.at[me_f])

    from_groups(0, lambda o: last_recv.at[o])
    get_wq.wait()
    query_part = dot(last_recv[:, 0, :].astype(BF16), wq[...])
    query_send[...] = folded(query_part)
    query_recv[f] = query_send[...]
    across_groups(3, lambda t: query_send, lambda me_f: query_recv.at[me_f])
    get_wk.wait()
    from_groups(3, lambda o: query_recv.at[o])
    query = unfolded(jnp.sum(query_recv[...].astype(F32), axis=0)).astype(BF16)

    gain_rows = attn_gain[:, pl.ds(pl.multiple_of(f * rows_per, rows_per), rows_per)]
    for h in range(local_heads):
        span = slice(h * HD, (h + 1) * HD)
        probe = dot_rows(query[:, span], wk[:, span]) * gain_rows
        for c in range(chunks):
            stage[:, c * local_heads + h, :] = probe[:, c * 128 : (c + 1) * 128]
    key_send[...] = stage[...].astype(BF16)
    home = lax.div(f, owners)
    inner = lax.rem(f, owners)
    at_home = home == s
    own_key = copy_of(4, 0, inner * seq_count + s, key_send.at[f], key_recv.at[inner, s], f, home)

    @pl.when(at_home)
    def _():
        key_recv[inner, s] = key_send[f]

    @pl.when(jnp.logical_not(at_home))
    def _():
        own_key.start()

    for k in range(1, groups):
        t = wrap(f + k, groups)
        push(4, k, inner * seq_count + s, key_send.at[t], key_recv.at[inner, s], t, home)

    tally = last_recv[:, 2, :128]
    tallies = jnp.concatenate([tally] * (slots // 128), axis=1)
    source_of = iota((groups, slots), 0)
    owner = lax.div(iota((groups, slots), 1), capacity)
    arrived = jnp.sum(jnp.where(source_of == owner, tallies, 0.0), axis=0, keepdims=True)
    offset = jnp.sum(jnp.where(source_of < owner, tallies, 0.0), axis=0, keepdims=True)
    within = lax.rem(iota((1, slots), 1), capacity).astype(F32)
    first = start[0].astype(F32)
    position = jnp.where(within < arrived, first + offset + within, -1.0)
    place = jnp.where(iota((seq_len, slots), 0).astype(F32) == position, 1.0, 0.0).astype(BF16)
    total = jnp.sum(tally[:, :1], axis=0, keepdims=True)
    row = iota((seq_len, 1), 0).astype(F32)
    taken = jnp.logical_and(row >= first, row < first + total)
    from_groups(2, lambda o: box_recv.at[o])
    step = min(256, piece)
    squares = jnp.zeros((seq_len, 1), F32)
    for c in range(piece // step):
        span = slice(c * step, (c + 1) * step)
        placed = dot(place, box_recv[:, :, span].reshape(slots, step))
        at = pl.multiple_of(s * piece + c * step, step)
        value = jnp.where(taken, placed, text[:, pl.ds(at, step)].astype(F32))
        states[:, span] = value.astype(BF16)
        squares = squares + jnp.sum(value * value, axis=1, keepdims=True)

    for b in range(owners):
        for k in range(seq_count):
            o = wrap(s + k, seq_count)
            if k:
                arrive(4, b * seq_count + o, key_recv.at[b, o])
            else:

                @pl.when(jnp.logical_not(f == s * owners + b))
                def _(o=o, b=b):
                    arrive(4, b * seq_count + o, key_recv.at[b, o])

    for o in range(seq_count):
        for b in range(owners):
            block = key_recv[b, o].astype(F32)
            for c in range(chunks):
                at = b * rows_per + c * 128
                heads_in[o * local_heads : (o + 1) * local_heads, at : at + 128] = block[
                    c * local_heads : (c + 1) * local_heads
                ]
    heads_in[heads:, :] = jnp.zeros((8, piece), F32)
    part = dot_rows(states[...], heads_in[...].astype(BF16))
    part = jnp.where(iota((1, heads + 8), 1) == heads, squares, part)
    score_recv[s] = part.T
    across_seq(5, lambda t: score_recv.at[s], lambda me_s: score_recv.at[me_s])
    from_seq(5, lambda o: score_recv.at[o])
    summed = jnp.sum(score_recv[...], axis=0)
    inverse = lax.rsqrt(summed[heads : heads + 1] / width + norm_epsilon)
    live = iota((1, seq_len), 1) < length
    scores = jnp.where(live, summed[:heads] * inverse / math.sqrt(HD), -jnp.inf)
    shifted = jnp.exp(scores - jnp.max(scores, axis=1, keepdims=True))
    weights = shifted / jnp.sum(shifted, axis=1, keepdims=True)
    mixed = dot((weights * inverse).astype(BF16), states[...])
    mixed = mixed * attn_gain[:, pl.ds(pl.multiple_of(s * piece, piece), piece)]

    for o in range(seq_count):
        for b in range(owners):
            rows = mixed[o * local_heads : (o + 1) * local_heads]
            starts = [b * rows_per + c * 128 for c in range(chunks)]
            mix_send[b, o] = jnp.concatenate(
                [rows[:, at : at + 128] for at in starts], axis=0
            ).astype(BF16)
    own_mix = []
    for b in range(owners):
        t = s * owners + b
        copy = copy_of(6, b * seq_count, f, mix_send.at[b, s], mix_recv.at[f], t, s)
        own_mix.append((t, copy))

        @pl.when(f == t)
        def _(b=b):
            mix_recv[f] = mix_send[b, s]

        @pl.when(jnp.logical_not(f == t))
        def _(copy=copy):
            copy.start()

        for k in range(1, seq_count):
            o = wrap(s + k, seq_count)
            push(6, b * seq_count + k, f, mix_send.at[b, o], mix_recv.at[f], t, o)
    get_wv.wait()
    from_groups(6, lambda o: mix_recv.at[o])

    @pl.when(jnp.logical_not(at_home))
    def _():
        arrive(6, f, mix_recv.at[f])

    stage[...] = mix_recv[...].astype(F32)
    att_part = []
    for h in range(local_heads):
        rows = [stage[:, c * local_heads + h, :] for c in range(chunks)]
        rows = jnp.concatenate(rows, axis=1).astype(BF16)
        att_part.append(dot(rows, wv[:, h * HD : (h + 1) * HD]))
    att_send[...] = folded(jnp.concatenate(att_part, axis=1))
    att_recv[f] = att_send[...]
    across_groups(7, lambda t: att_send, lambda me_f: att_recv.at[me_f])
    get_wo.wait()
    from_groups(7, lambda o: att_recv.at[o])
    attended = unfolded(jnp.sum(att_recv[...].astype(F32), axis=0)).astype(BF16)

    out_recv[s] = dot(attended, wo[...])
    across_seq(8, lambda t: out_recv.at[s], lambda me_s: out_recv.at[me_s])
    from_seq(8, lambda o: out_recv.at[o])
    residual = last_recv[:, 1, :] + jnp.sum(out_recv[...], axis=0)
    square_part = jnp.sum(residual * residual, axis=1, keepdims=True)
    final_rows = final_gain[:, pl.ds(pl.multiple_of(f * rows_per, rows_per), rows_per)]
    scaled = residual * final_rows
    scaled_send[...] = folded(scaled)

    scaled_recv[f] = scaled_send[...]
    across_groups(9, lambda t: scaled_send, lambda me_f: scaled_recv.at[me_f])

    @pl.when(jnp.logical_not(final_seq))
    def _():
        get_lm.wait()

    @pl.when(final_seq)
    def _():
        get_lm_final.wait()

    logits = jnp.zeros((groups, words), F32)
    for k in range(groups):
        o = wrap(f + groups - k, groups)
        if k:
            arrive(9, o, scaled_recv.at[o])
        for c in range(2):
            at = pl.multiple_of(o * rows_per + c * half, half)
            logits = logits + dot_rows(
                scaled_recv[o, c * groups : (c + 1) * groups, :], lm[:, pl.ds(at, half)]
            )
    word = iota((1, words), 1) + s * words
    top = jnp.max(jnp.where(word < vocab, logits, -jnp.inf), axis=1, keepdims=True)
    peaks = jnp.where(iota((groups, 128), 1) < 64, top, square_part)
    for o in range(seq_count):
        peak_send[o] = peaks[o * owners : (o + 1) * owners]
    peak_row[s] = peak_send[s]
    across_seq(10, lambda t: peak_send.at[t], lambda me_s: peak_row.at[me_s])
    from_seq(10, lambda o: peak_row.at[o])
    lane = iota((owners, 128), 1)
    peak_recv[f] = jnp.where(lane < 64, jnp.max(peak_row[...], axis=0), peak_row[0])
    across_groups(11, lambda t: peak_recv.at[f], lambda me_f: peak_recv.at[me_f])
    from_groups(11, lambda o: peak_recv.at[o])
    everyone = peak_recv[...]
    best = jnp.max(everyone, axis=0)[:, :1]
    mean_square = jnp.sum(everyone, axis=0)[:, 64:65] / width
    rms_out[...] = jnp.broadcast_to(jnp.sqrt(mean_square), (owners, 128))
    max_out[...] = jnp.broadcast_to(best * lax.rsqrt(mean_square + norm_epsilon), (owners, 128))

    for copy in sent:
        copy.wait_send()

    @pl.when(jnp.logical_not(at_home))
    def _():
        own_key.wait_send()

    for t, copy in own_mix:

        @pl.when(jnp.logical_not(f == t))
        def _(copy=copy):
            copy.wait_send()


def fused(
    text_embeds,
    vision_tokens,
    vision_request,
    image_start,
    lengths,
    attn_gain,
    w_query,
    w_key,
    w_value,
    w_out,
    final_gain,
    lm_head,
):
    groups = lax.axis_size("fsdp")
    seq_count = lax.axis_size("seq")
    seq_len, width = text_embeds.shape
    vtok, piece = vision_tokens.shape
    rows_per, columns = w_query.shape
    words = -(-lm_head.shape[1] // (16 * seq_count)) * 16
    owners = groups // seq_count
    local_heads = columns // HD
    heads = local_heads * seq_count
    capacity = 2 * vtok // groups
    vmem = pl.BlockSpec(memory_space=pltpu.VMEM)
    smem = pl.BlockSpec(memory_space=pltpu.SMEM)
    any_space = pl.BlockSpec(memory_space=pl.ANY)
    phases = 12
    links = max(groups, owners * seq_count)
    rms, best = pl.pallas_call(
        functools.partial(fused_kernel, groups, seq_count, capacity),
        out_shape=[jax.ShapeDtypeStruct((owners, 128), F32)] * 2,
        in_specs=[vmem, smem, smem, vmem, vmem] + [any_space] * 7,
        out_specs=[vmem, vmem],
        scratch_shapes=[
            pltpu.VMEM((seq_len, width), BF16),
            pltpu.VMEM((vtok, piece), BF16),
            pltpu.VMEM((rows_per, columns), BF16),
            pltpu.VMEM((rows_per, columns), BF16),
            pltpu.VMEM((rows_per, columns), BF16),
            pltpu.VMEM((columns, rows_per), BF16),
            pltpu.VMEM((words, width), BF16),
            pltpu.VMEM((seq_len, piece), BF16),
            pltpu.VMEM((heads + 8, piece), F32),
            pltpu.VMEM((groups, local_heads * rows_per // 128, 128), F32),
            pltpu.VMEM((groups, 3, rows_per), F32),
            pltpu.VMEM((groups, 3, rows_per), F32),
            pltpu.VMEM((groups, capacity, piece), BF16),
            pltpu.VMEM((groups, capacity, piece), BF16),
            pltpu.VMEM((2 * groups, columns // 2), BF16),
            pltpu.VMEM((groups, 2 * groups, columns // 2), BF16),
            pltpu.VMEM((groups, local_heads * rows_per // 128, 128), BF16),
            pltpu.VMEM((owners, seq_count, local_heads * rows_per // 128, 128), BF16),
            pltpu.VMEM((seq_count, heads + 8, seq_len), F32),
            pltpu.VMEM((owners, seq_count, local_heads * rows_per // 128, 128), BF16),
            pltpu.VMEM((groups, local_heads * rows_per // 128, 128), BF16),
            pltpu.VMEM((2 * groups, columns // 2), BF16),
            pltpu.VMEM((groups, 2 * groups, columns // 2), BF16),
            pltpu.VMEM((seq_count, groups, rows_per), F32),
            pltpu.VMEM((2 * groups, rows_per // 2), BF16),
            pltpu.VMEM((groups, 2 * groups, rows_per // 2), BF16),
            pltpu.VMEM((seq_count, owners, 128), F32),
            pltpu.VMEM((seq_count, owners, 128), F32),
            pltpu.VMEM((groups, owners, 128), F32),
            pltpu.SemaphoreType.DMA((7,)),
            pltpu.SemaphoreType.DMA((phases, links)),
            pltpu.SemaphoreType.DMA((phases, links)),
        ],
        compiler_params=pltpu.CompilerParams(
            collective_id=0, has_side_effects=True, vmem_limit_bytes=56 * 2**20
        ),
        name="fused",
    )(
        vision_request.reshape(1, vtok),
        image_start,
        lengths,
        attn_gain.reshape(1, width),
        final_gain.reshape(1, width),
        text_embeds,
        vision_tokens,
        w_query,
        w_key,
        w_value,
        w_out,
        lm_head.T,
    )
    return rms[:, 0], best[:, 0]


def fits(mesh):
    groups, seq_count = mesh.shape["fsdp"], mesh.shape["seq"]
    return groups == 8 and groups % seq_count == 0


def solution(mesh):
    return jax.shard_map(
        fused if fits(mesh) else local,
        mesh=mesh,
        in_specs=(
            P("fsdp", None),
            P("fsdp", "seq"),
            P("fsdp", None),
            P("fsdp"),
            P("fsdp"),
            P(),
            P("fsdp", "seq"),
            P("fsdp", "seq"),
            P("fsdp", "seq"),
            P(None, "fsdp"),
            P(),
            P(None, "fsdp"),
        ),
        out_specs=(P("seq"), P("seq")),
        check_vma=False,
    )
```

```python
import functools
import math

import jax
import jax.numpy as jnp
from jax import lax
from jax.experimental import pallas as pl
from jax.experimental.pallas import tpu as pltpu
from jax.sharding import PartitionSpec as P

HD = 128


norm_epsilon = 1e-05


def row_norm(rows, gain):
    widened = rows.astype(jnp.float32)
    return (
        widened
        * lax.rsqrt(jnp.mean(widened * widened, axis=1, keepdims=True) + norm_epsilon)
        * gain
    ).astype(jnp.bfloat16)


def pack_slots(tokens, destination, slot_index, groups, capacity):
    return (
        jnp.zeros((groups, capacity, tokens.shape[1]), jnp.bfloat16)
        .at[destination, slot_index]
        .set(tokens)
    )


def local(
    text_embeds,
    vision_tokens,
    vision_request,
    image_start,
    lengths,
    attn_gain,
    w_query,
    w_key,
    w_value,
    w_out,
    final_gain,
    lm_head,
):
    groups = lax.axis_size("fsdp")
    seq_count = lax.axis_size("seq")
    group_index = lax.axis_index("fsdp")
    seq_index = lax.axis_index("seq")
    seq_len = text_embeds.shape[0]
    width = text_embeds.shape[1]
    columns = w_key.shape[1]
    heads_local = columns // HD
    dpiece = width // groups
    fpiece = width // seq_count
    quarter = groups // seq_count
    capacity = max(2, 2 * vision_tokens.shape[0] // groups)
    last_index = lengths[0] - 1
    destination = vision_request[:, 0]
    onehot = (destination[:, None] == jnp.arange(groups, dtype=jnp.int32)[None, :]).astype(
        jnp.int32
    )
    slot_index = jnp.sum((jnp.cumsum(onehot, axis=0) - onehot) * onehot, axis=1)
    counts = jnp.sum(onehot, axis=0)
    outbox = pack_slots(vision_tokens, destination, slot_index, groups, capacity)
    final_text = lax.dynamic_slice_in_dim(text_embeds, last_index, 1, 0)
    last_row = row_norm(final_text, attn_gain)
    last_pieces = jnp.stack(
        [last_row.reshape(groups, dpiece), final_text.reshape(groups, dpiece)], axis=1
    )
    last_parts = lax.all_to_all(last_pieces, "fsdp", split_axis=0, concat_axis=0, tiled=True)
    received = lax.all_to_all(outbox, "fsdp", split_axis=0, concat_axis=0, tiled=True)
    arrived = lax.all_to_all(counts[:, None], "fsdp", split_axis=0, concat_axis=0, tiled=True)
    query = lax.psum(
        jnp.dot(last_parts[:, 0], w_query, preferred_element_type=jnp.float32), "fsdp"
    ).astype(jnp.bfloat16)
    gain_part = lax.dynamic_slice_in_dim(attn_gain, group_index * dpiece, dpiece, 0)
    probe_part = (
        jnp.einsum(
            "rhc,dhc->rhd",
            query.reshape(groups, heads_local, HD),
            w_key.reshape(dpiece, heads_local, HD),
            preferred_element_type=jnp.float32,
        )
        * gain_part
    ).astype(jnp.bfloat16)
    probe = lax.all_to_all(probe_part, "fsdp", split_axis=0, concat_axis=0, tiled=True)
    probe = probe.transpose(1, 0, 2).reshape(heads_local, width)
    probe = lax.all_to_all(probe, "seq", split_axis=1, concat_axis=0, tiled=True)
    occupied = (
        (jnp.arange(capacity, dtype=jnp.int32)[None, :] < arrived).astype(jnp.int32).reshape(-1)
    )
    ranking = jnp.cumsum(occupied) - occupied
    positions = jnp.where(occupied > 0, image_start[0] + ranking, seq_len)
    text_piece = lax.dynamic_slice_in_dim(text_embeds, seq_index * fpiece, fpiece, 1)
    states = text_piece.at[positions].set(received.reshape(-1, fpiece), mode="drop")
    widened = states.astype(jnp.float32)
    squares = jnp.sum(widened * widened, axis=1)
    partial_scores = jnp.einsum("hd,jd->hj", probe, states, preferred_element_type=jnp.float32)
    summed = lax.psum(jnp.concatenate([partial_scores, squares[None, :]], axis=0), "seq")
    inverse = lax.rsqrt(summed[-1:] / width + norm_epsilon)
    scores = summed[:-1] * inverse / math.sqrt(HD)
    live_keys = jnp.arange(seq_len, dtype=jnp.int32) < lengths[0]
    scores = jnp.where(live_keys[None, :], scores, -jnp.inf)
    peak = jnp.max(scores, axis=1, keepdims=True)
    shifted = jnp.exp(scores - peak)
    weights = shifted / jnp.sum(shifted, axis=1, keepdims=True)
    mixed = jnp.dot(
        (weights * inverse).astype(jnp.bfloat16), states, preferred_element_type=jnp.float32
    )
    mixed_gain = lax.dynamic_slice_in_dim(attn_gain, seq_index * fpiece, fpiece, 0)
    mixed = (mixed * mixed_gain).astype(jnp.bfloat16)
    mixed = lax.all_to_all(mixed, "seq", split_axis=0, concat_axis=1, tiled=True)
    mixed = mixed.reshape(heads_local, groups, dpiece).transpose(1, 0, 2)
    mixed = lax.all_to_all(mixed, "fsdp", split_axis=0, concat_axis=0, tiled=True)
    attended = lax.psum(
        jnp.einsum(
            "rhd,dhc->rhc",
            mixed,
            w_value.reshape(dpiece, heads_local, HD),
            preferred_element_type=jnp.float32,
        ).reshape(groups, columns),
        "fsdp",
    ).astype(jnp.bfloat16)
    out_rows = lax.dynamic_slice_in_dim(w_out, seq_index * columns, columns, 0)
    projected = lax.psum(jnp.dot(attended, out_rows, preferred_element_type=jnp.float32), "seq")
    residual_out = last_parts[:, 1].astype(jnp.float32) + projected
    residual_out = lax.dynamic_slice_in_dim(residual_out, seq_index * quarter, quarter, 0)
    final_part = lax.dynamic_slice_in_dim(final_gain, group_index * dpiece, dpiece, 0)
    scaled_out = (residual_out * final_part[None, :]).astype(jnp.bfloat16)
    square_part = jnp.sum(residual_out * residual_out, axis=1)
    full_scaled = lax.all_gather(scaled_out, "fsdp", axis=1, tiled=True)
    mean_square = lax.psum(square_part, "fsdp") / width
    logits = jnp.dot(full_scaled, lm_head, preferred_element_type=jnp.float32)
    local_max = jnp.max(logits, axis=1) * lax.rsqrt(mean_square + norm_epsilon)
    max_logit = lax.pmax(local_max, "fsdp")
    return (jnp.sqrt(mean_square), max_logit)


MESH = pl.DeviceIdType.MESH
F32 = jnp.float32
BF16 = jnp.bfloat16


def dot(a, b):
    return jnp.dot(a, b, preferred_element_type=F32)


def dot_rows(a, b):
    return lax.dot_general(a, b, (((1,), (1,)), ((), ())), preferred_element_type=F32)


def iota(shape, axis):
    return lax.broadcasted_iota(jnp.int32, shape, axis)


def folded(rows):
    half = rows.shape[1] // 2
    return jnp.concatenate([rows[:, :half], rows[:, half:]], axis=0).astype(BF16)


def unfolded(rows):
    half = rows.shape[0] // 2
    return jnp.concatenate([rows[:half], rows[half:]], axis=1)


def wrap(index, size):
    return jnp.where(index >= size, index - size, index)


def fused_kernel(
    groups,
    seq_count,
    capacity,
    request,
    start,
    lengths,
    attn_gain,
    final_gain,
    text_hbm,
    vision_hbm,
    wq_hbm,
    wk_hbm,
    wv_hbm,
    wo_hbm,
    lm_hbm,
    rms_out,
    max_out,
    text,
    vision,
    wq,
    wk,
    wv,
    wo,
    lm,
    states,
    heads_in,
    stage,
    last_send,
    last_recv,
    box_send,
    box_recv,
    query_send,
    query_recv,
    key_send,
    key_recv,
    score_recv,
    mix_send,
    mix_recv,
    att_send,
    att_recv,
    out_recv,
    scaled_send,
    scaled_recv,
    peak_send,
    peak_row,
    peak_recv,
    local_sem,
    send_sem,
    recv_sem,
):
    f = lax.axis_index("fsdp")
    s = lax.axis_index("seq")
    devices = groups * seq_count
    seq_len, width = text.shape
    rows_per = width // groups
    piece = width // seq_count
    owners = groups // seq_count
    columns = wq.shape[1]
    local_heads = columns // HD
    heads = local_heads * seq_count
    vtok = vision.shape[0]
    half = rows_per // 2
    chunks = rows_per // 128

    barrier = pltpu.get_barrier_semaphore()
    me = f * seq_count + s

    others = []
    for k in range(groups):
        for j in range(seq_count):
            if k or j:
                others.append((wrap(f + k, groups), wrap(s + j, seq_count)))

    def fetch(index, source, target):
        copy = pltpu.make_async_copy(source, target, local_sem.at[index])
        copy.start()
        return copy

    get_text = fetch(0, text_hbm, text)
    get_vision = fetch(1, vision_hbm, vision)
    for other in others:
        pl.semaphore_signal(barrier, inc=1, device_id=other, device_id_type=MESH)
    get_wq = fetch(2, wq_hbm, wq)
    get_wk = fetch(3, wk_hbm, wk)

    sent = []

    def copy_of(phase, slot, from_slot, source, target, to_f, to_s):
        return pltpu.make_async_remote_copy(
            src_ref=source,
            dst_ref=target,
            send_sem=send_sem.at[phase, slot],
            recv_sem=recv_sem.at[phase, from_slot],
            device_id=(to_f, to_s),
            device_id_type=MESH,
        )

    def push(*what):
        copy = copy_of(*what)
        copy.start()
        sent.append(copy)

    def arrive(phase, slot, target):
        copy_of(phase, 0, slot, target, target, f, s).wait_recv()

    def across_groups(phase, source, target):
        for k in range(1, groups):
            t = wrap(f + k, groups)
            push(phase, k, f, source(t), target(f), t, s)

    def from_groups(phase, target):
        for k in range(1, groups):
            o = wrap(f + groups - k, groups)
            arrive(phase, o, target(o))

    def across_seq(phase, source, target):
        for k in range(1, seq_count):
            t = wrap(s + k, seq_count)
            push(phase, k, s, source(t), target(s), f, t)

    def from_seq(phase, target):
        for k in range(1, seq_count):
            o = wrap(s + seq_count - k, seq_count)
            arrive(phase, o, target(o))

    length = lengths[0]
    tail = (seq_len - 8) // 16 * 16
    get_text.wait()
    get_wv = fetch(4, wv_hbm, wv)
    get_wo = fetch(5, wo_hbm.at[pl.ds(pl.multiple_of(s * columns, columns), columns)], wo)
    words = lm.shape[0]
    vocab = lm_hbm.shape[0]
    final_seq = s == seq_count - 1
    final_words = vocab - (seq_count - 1) * words
    get_lm = pltpu.make_async_copy(
        lm_hbm.at[pl.ds(pl.multiple_of(s * words, words), words)], lm, local_sem.at[6]
    )
    get_lm_final = pltpu.make_async_copy(
        lm_hbm.at[vocab - final_words :], lm.at[:final_words], local_sem.at[6]
    )

    @pl.when(jnp.logical_not(final_seq))
    def _():
        get_lm.start()

    @pl.when(final_seq)
    def _():
        get_lm_final.start()
        if final_words < words:
            lm[final_words:, :] = jnp.zeros((words - final_words, width), BF16)

    tail_rows = text[tail:, :].astype(F32)
    here = iota((seq_len - tail, 1), 0) == length - 1 - tail
    last = jnp.sum(jnp.where(here, tail_rows, 0.0), axis=0, keepdims=True)
    scale = lax.rsqrt(jnp.mean(last * last, axis=1, keepdims=True) + norm_epsilon)
    normed = (last * scale * attn_gain[...]).astype(BF16).astype(F32)
    named = request[...]
    member = jnp.where(iota((groups, vtok), 0) == named, 1.0, 0.0)
    counts = jnp.broadcast_to(jnp.sum(member, axis=1, keepdims=True), (groups, rows_per))
    for g in range(groups):
        span = slice(g * rows_per, (g + 1) * rows_per)
        last_send[g, 0:1, :] = normed[:, span]
        last_send[g, 1:2, :] = last[:, span]
        last_send[g, 2:3, :] = counts[g : g + 1, :]
    last_recv[f] = last_send[f]

    earlier = jnp.where(iota((vtok, vtok), 0) < iota((vtok, vtok), 1), 1.0, 0.0)
    before = dot(member.astype(BF16), earlier.astype(BF16))
    rank = jnp.sum(before * member, axis=0, keepdims=True)
    slot = named.astype(F32) * capacity + rank
    slots = groups * capacity
    pick = jnp.where(iota((slots, vtok), 0).astype(F32) == slot, 1.0, 0.0).astype(BF16)
    get_vision.wait()
    box_send[...] = dot(pick, vision[...]).astype(BF16).reshape(groups, capacity, piece)
    box_recv[f] = box_send[f]
    pl.semaphore_wait(barrier, devices - 1)
    across_groups(0, lambda t: last_send.at[t], lambda me_f: last_recv.at[me_f])

    across_groups(2, lambda t: box_send.at[t], lambda me_f: box_recv.at[me_f])

    from_groups(0, lambda o: last_recv.at[o])
    get_wq.wait()
    query_part = dot(last_recv[:, 0, :].astype(BF16), wq[...])
    query_send[...] = folded(query_part)
    query_recv[f] = query_send[...]
    across_groups(3, lambda t: query_send, lambda me_f: query_recv.at[me_f])
    get_wk.wait()
    from_groups(3, lambda o: query_recv.at[o])
    query = unfolded(jnp.sum(query_recv[...].astype(F32), axis=0)).astype(BF16)

    gain_rows = attn_gain[:, pl.ds(pl.multiple_of(f * rows_per, rows_per), rows_per)]
    for h in range(local_heads):
        span = slice(h * HD, (h + 1) * HD)
        probe = dot_rows(query[:, span], wk[:, span]) * gain_rows
        for c in range(chunks):
            stage[:, c * local_heads + h, :] = probe[:, c * 128 : (c + 1) * 128]
    key_send[...] = stage[...].astype(BF16)
    home = lax.div(f, owners)
    inner = lax.rem(f, owners)
    at_home = home == s
    own_key = copy_of(4, 0, inner * seq_count + s, key_send.at[f], key_recv.at[inner, s], f, home)

    @pl.when(at_home)
    def _():
        key_recv[inner, s] = key_send[f]

    @pl.when(jnp.logical_not(at_home))
    def _():
        own_key.start()

    for k in range(1, groups):
        t = wrap(f + k, groups)
        push(4, k, inner * seq_count + s, key_send.at[t], key_recv.at[inner, s], t, home)

    tally = last_recv[:, 2, :128]
    tallies = jnp.concatenate([tally] * (slots // 128), axis=1)
    source_of = iota((groups, slots), 0)
    owner = lax.div(iota((groups, slots), 1), capacity)
    arrived = jnp.sum(jnp.where(source_of == owner, tallies, 0.0), axis=0, keepdims=True)
    offset = jnp.sum(jnp.where(source_of < owner, tallies, 0.0), axis=0, keepdims=True)
    within = lax.rem(iota((1, slots), 1), capacity).astype(F32)
    first = start[0].astype(F32)
    position = jnp.where(within < arrived, first + offset + within, -1.0)
    place = jnp.where(iota((seq_len, slots), 0).astype(F32) == position, 1.0, 0.0).astype(BF16)
    total = jnp.sum(tally[:, :1], axis=0, keepdims=True)
    row = iota((seq_len, 1), 0).astype(F32)
    taken = jnp.logical_and(row >= first, row < first + total)
    from_groups(2, lambda o: box_recv.at[o])
    step = min(256, piece)
    squares = jnp.zeros((seq_len, 1), F32)
    for c in range(piece // step):
        span = slice(c * step, (c + 1) * step)
        placed = dot(place, box_recv[:, :, span].reshape(slots, step))
        at = pl.multiple_of(s * piece + c * step, step)
        value = jnp.where(taken, placed, text[:, pl.ds(at, step)].astype(F32))
        states[:, span] = value.astype(BF16)
        squares = squares + jnp.sum(value * value, axis=1, keepdims=True)

    for b in range(owners):
        for k in range(seq_count):
            o = wrap(s + k, seq_count)
            if k:
                arrive(4, b * seq_count + o, key_recv.at[b, o])
            else:

                @pl.when(jnp.logical_not(f == s * owners + b))
                def _(o=o, b=b):
                    arrive(4, b * seq_count + o, key_recv.at[b, o])

    for o in range(seq_count):
        for b in range(owners):
            block = key_recv[b, o].astype(F32)
            for c in range(chunks):
                at = b * rows_per + c * 128
                heads_in[o * local_heads : (o + 1) * local_heads, at : at + 128] = block[
                    c * local_heads : (c + 1) * local_heads
                ]
    heads_in[heads:, :] = jnp.zeros((8, piece), F32)
    part = dot_rows(states[...], heads_in[...].astype(BF16))
    part = jnp.where(iota((1, heads + 8), 1) == heads, squares, part)
    score_recv[s] = part.T
    across_seq(5, lambda t: score_recv.at[s], lambda me_s: score_recv.at[me_s])
    from_seq(5, lambda o: score_recv.at[o])
    summed = jnp.sum(score_recv[...], axis=0)
    inverse = lax.rsqrt(summed[heads : heads + 1] / width + norm_epsilon)
    live = iota((1, seq_len), 1) < length
    scores = jnp.where(live, summed[:heads] * inverse / math.sqrt(HD), -jnp.inf)
    shifted = jnp.exp(scores - jnp.max(scores, axis=1, keepdims=True))
    weights = shifted / jnp.sum(shifted, axis=1, keepdims=True)
    mixed = dot((weights * inverse).astype(BF16), states[...])
    mixed = mixed * attn_gain[:, pl.ds(pl.multiple_of(s * piece, piece), piece)]

    for o in range(seq_count):
        for b in range(owners):
            rows = mixed[o * local_heads : (o + 1) * local_heads]
            starts = [b * rows_per + c * 128 for c in range(chunks)]
            mix_send[b, o] = jnp.concatenate(
                [rows[:, at : at + 128] for at in starts], axis=0
            ).astype(BF16)
    own_mix = []
    for b in range(owners):
        t = s * owners + b
        copy = copy_of(6, b * seq_count, f, mix_send.at[b, s], mix_recv.at[f], t, s)
        own_mix.append((t, copy))

        @pl.when(f == t)
        def _(b=b):
            mix_recv[f] = mix_send[b, s]

        @pl.when(jnp.logical_not(f == t))
        def _(copy=copy):
            copy.start()

        for k in range(1, seq_count):
            o = wrap(s + k, seq_count)
            push(6, b * seq_count + k, f, mix_send.at[b, o], mix_recv.at[f], t, o)
    get_wv.wait()
    from_groups(6, lambda o: mix_recv.at[o])

    @pl.when(jnp.logical_not(at_home))
    def _():
        arrive(6, f, mix_recv.at[f])

    stage[...] = mix_recv[...].astype(F32)
    att_part = []
    for h in range(local_heads):
        rows = [stage[:, c * local_heads + h, :] for c in range(chunks)]
        rows = jnp.concatenate(rows, axis=1).astype(BF16)
        att_part.append(dot(rows, wv[:, h * HD : (h + 1) * HD]))
    att_send[...] = folded(jnp.concatenate(att_part, axis=1))
    att_recv[f] = att_send[...]
    across_groups(7, lambda t: att_send, lambda me_f: att_recv.at[me_f])
    get_wo.wait()
    from_groups(7, lambda o: att_recv.at[o])
    attended = unfolded(jnp.sum(att_recv[...].astype(F32), axis=0)).astype(BF16)

    out_recv[s] = dot(attended, wo[...])
    across_seq(8, lambda t: out_recv.at[s], lambda me_s: out_recv.at[me_s])
    from_seq(8, lambda o: out_recv.at[o])
    residual = last_recv[:, 1, :] + jnp.sum(out_recv[...], axis=0)
    square_part = jnp.sum(residual * residual, axis=1, keepdims=True)
    final_rows = final_gain[:, pl.ds(pl.multiple_of(f * rows_per, rows_per), rows_per)]
    scaled = residual * final_rows
    scaled_send[...] = folded(scaled)

    scaled_recv[f] = scaled_send[...]
    across_groups(9, lambda t: scaled_send, lambda me_f: scaled_recv.at[me_f])

    @pl.when(jnp.logical_not(final_seq))
    def _():
        get_lm.wait()

    @pl.when(final_seq)
    def _():
        get_lm_final.wait()

    logits = jnp.zeros((groups, words), F32)
    for k in range(groups):
        o = wrap(f + groups - k, groups)
        if k:
            arrive(9, o, scaled_recv.at[o])
        for c in range(2):
            at = pl.multiple_of(o * rows_per + c * half, half)
            logits = logits + dot_rows(
                scaled_recv[o, c * groups : (c + 1) * groups, :], lm[:, pl.ds(at, half)]
            )
    word = iota((1, words), 1) + s * words
    top = jnp.max(jnp.where(word < vocab, logits, -jnp.inf), axis=1, keepdims=True)
    peaks = jnp.where(iota((groups, 128), 1) < 64, top, square_part)
    for o in range(seq_count):
        peak_send[o] = peaks[o * owners : (o + 1) * owners]
    peak_row[s] = peak_send[s]
    across_seq(10, lambda t: peak_send.at[t], lambda me_s: peak_row.at[me_s])
    from_seq(10, lambda o: peak_row.at[o])
    lane = iota((owners, 128), 1)
    peak_recv[f] = jnp.where(lane < 64, jnp.max(peak_row[...], axis=0), peak_row[0])
    settled = len(sent)
    across_groups(11, lambda t: peak_recv.at[f], lambda me_f: peak_recv.at[me_f])
    for copy in sent[:settled]:
        copy.wait_send()

    @pl.when(jnp.logical_not(at_home))
    def _():
        own_key.wait_send()

    for t, copy in own_mix:

        @pl.when(jnp.logical_not(f == t))
        def _(copy=copy):
            copy.wait_send()

    from_groups(11, lambda o: peak_recv.at[o])
    everyone = peak_recv[...]
    best = jnp.max(everyone, axis=0)[:, :1]
    mean_square = jnp.sum(everyone, axis=0)[:, 64:65] / width
    rms_out[...] = jnp.broadcast_to(jnp.sqrt(mean_square), (owners, 128))
    max_out[...] = jnp.broadcast_to(best * lax.rsqrt(mean_square + norm_epsilon), (owners, 128))

    for copy in sent[settled:]:
        copy.wait_send()


def fused(
    text_embeds,
    vision_tokens,
    vision_request,
    image_start,
    lengths,
    attn_gain,
    w_query,
    w_key,
    w_value,
    w_out,
    final_gain,
    lm_head,
):
    groups = lax.axis_size("fsdp")
    seq_count = lax.axis_size("seq")
    seq_len, width = text_embeds.shape
    vtok, piece = vision_tokens.shape
    rows_per, columns = w_query.shape
    words = -(-lm_head.shape[1] // (16 * seq_count)) * 16
    owners = groups // seq_count
    local_heads = columns // HD
    heads = local_heads * seq_count
    capacity = 2 * vtok // groups
    vmem = pl.BlockSpec(memory_space=pltpu.VMEM)
    smem = pl.BlockSpec(memory_space=pltpu.SMEM)
    any_space = pl.BlockSpec(memory_space=pl.ANY)
    phases = 12
    links = max(groups, owners * seq_count)
    rms, best = pl.pallas_call(
        functools.partial(fused_kernel, groups, seq_count, capacity),
        out_shape=[jax.ShapeDtypeStruct((owners, 128), F32)] * 2,
        in_specs=[vmem, smem, smem, vmem, vmem] + [any_space] * 7,
        out_specs=[vmem, vmem],
        scratch_shapes=[
            pltpu.VMEM((seq_len, width), BF16),
            pltpu.VMEM((vtok, piece), BF16),
            pltpu.VMEM((rows_per, columns), BF16),
            pltpu.VMEM((rows_per, columns), BF16),
            pltpu.VMEM((rows_per, columns), BF16),
            pltpu.VMEM((columns, rows_per), BF16),
            pltpu.VMEM((words, width), BF16),
            pltpu.VMEM((seq_len, piece), BF16),
            pltpu.VMEM((heads + 8, piece), F32),
            pltpu.VMEM((groups, local_heads * rows_per // 128, 128), F32),
            pltpu.VMEM((groups, 3, rows_per), F32),
            pltpu.VMEM((groups, 3, rows_per), F32),
            pltpu.VMEM((groups, capacity, piece), BF16),
            pltpu.VMEM((groups, capacity, piece), BF16),
            pltpu.VMEM((2 * groups, columns // 2), BF16),
            pltpu.VMEM((groups, 2 * groups, columns // 2), BF16),
            pltpu.VMEM((groups, local_heads * rows_per // 128, 128), BF16),
            pltpu.VMEM((owners, seq_count, local_heads * rows_per // 128, 128), BF16),
            pltpu.VMEM((seq_count, heads + 8, seq_len), F32),
            pltpu.VMEM((owners, seq_count, local_heads * rows_per // 128, 128), BF16),
            pltpu.VMEM((groups, local_heads * rows_per // 128, 128), BF16),
            pltpu.VMEM((2 * groups, columns // 2), BF16),
            pltpu.VMEM((groups, 2 * groups, columns // 2), BF16),
            pltpu.VMEM((seq_count, groups, rows_per), F32),
            pltpu.VMEM((2 * groups, rows_per // 2), BF16),
            pltpu.VMEM((groups, 2 * groups, rows_per // 2), BF16),
            pltpu.VMEM((seq_count, owners, 128), F32),
            pltpu.VMEM((seq_count, owners, 128), F32),
            pltpu.VMEM((groups, owners, 128), F32),
            pltpu.SemaphoreType.DMA((7,)),
            pltpu.SemaphoreType.DMA((phases, links)),
            pltpu.SemaphoreType.DMA((phases, links)),
        ],
        compiler_params=pltpu.CompilerParams(
            collective_id=0, has_side_effects=True, vmem_limit_bytes=56 * 2**20
        ),
        name="fused",
    )(
        vision_request.reshape(1, vtok),
        image_start,
        lengths,
        attn_gain.reshape(1, width),
        final_gain.reshape(1, width),
        text_embeds,
        vision_tokens,
        w_query,
        w_key,
        w_value,
        w_out,
        lm_head.T,
    )
    return rms[:, 0], best[:, 0]


def fits(mesh):
    groups, seq_count = mesh.shape["fsdp"], mesh.shape["seq"]
    return groups == 8 and groups % seq_count == 0


def solution(mesh):
    return jax.shard_map(
        fused if fits(mesh) else local,
        mesh=mesh,
        in_specs=(
            P("fsdp", None),
            P("fsdp", "seq"),
            P("fsdp", None),
            P("fsdp"),
            P("fsdp"),
            P(),
            P("fsdp", "seq"),
            P("fsdp", "seq"),
            P("fsdp", "seq"),
            P(None, "fsdp"),
            P(),
            P(None, "fsdp"),
        ),
        out_specs=(P("seq"), P("seq")),
        check_vma=False,
    )
```
